512 devices in a mesh: dp: 8 (over z_lo, core), ctx: 64 (over x, y, z_hi).
Axes of the slice: x: 4, y: 8, z: 8 (z_hi: 2, z_lo: 4; z = z_hi * 4 + z_lo), core: 2. Of those that a mesh axis runs over, the one named last changes fastest.
Arguments:
- offsets: int32 [8], P('dp'), may hold values from 0 to 8176, as said below
- lengths: int32 [8], P('dp'), may hold values from 4 to 8192, as said below
- queries: bfloat16 [8, 16, 64, 576], P('dp', None, 'ctx'), may hold values from -2000 to 2000
- cotangent: bfloat16 [8, 16, 64, 512], P('dp', None, 'ctx'), may hold values from -6 to 6
- kv_rows: bfloat16 [8, 8192, 576], P('dp', 'ctx'), may hold values from -400 to 400
- kv_tangent: bfloat16 [8, 8192, 576], P('dp', 'ctx'), may hold values from -6 to 6
- norm_gain: float32 [512], replicated, may hold values from 0.5 to 1.5
- gain_tangent: float32 [512], replicated, may hold values from -6 to 6
Outputs:
- hv_rows: float32 [8, 8192, 576], P('dp', 'ctx')
- gain_pair: float32 [2, 512], replicated
The draws below stay inside these ranges and needn't reach their ends.
Inputs may be any that keep to these rules, and one draw needn't show every extreme that they name: offsets[d] + 16 <= 8192. lengths[d] - offsets[d] lies between 4 and 16.
All inputs are finite; a program needn't handle non-finite values.
Results may differ from the reference program's by a relative error of at most 0.0067.
Values may be sent and summed in bfloat16 or wider, within the bound.
No kernel may reach another device: no remote copies, remote signals or barrier semaphores. Data moves between devices by JAX's collectives and lax.ppermute only.
A program may use at most 64 MiB of HBM per device.

```python
import math
import jax
import jax.numpy as jnp
from jax import lax

LATENT = 512
ROPE = 64
HEADS = 64
SLAB = 16
CONTEXT = 8192
DOCS = 8


def slab_bounds(key):
    first_key, second_key, third_key = jax.random.split(key, 3)
    doc_index = jnp.arange(DOCS, dtype=jnp.int32)
    chosen = jax.random.randint(third_key, (), 0, DOCS, dtype=jnp.int32)
    starts = jax.random.randint(first_key, (DOCS,), 0, CONTEXT - SLAB + 1, dtype=jnp.int32)
    extents = jax.random.randint(second_key, (DOCS,), SLAB // 4, SLAB + 1, dtype=jnp.int32)
    starts = jnp.where(doc_index == chosen, CONTEXT - SLAB, starts)
    extents = jnp.where(doc_index == chosen, SLAB, extents)
    return (starts, starts + extents)


def latent_base(key):
    first_key, second_key, third_key = jax.random.split(key, 3)
    values = jax.random.normal(first_key, (DOCS, CONTEXT, LATENT + ROPE), jnp.float32)
    row_scale = jnp.exp(jax.random.uniform(second_key, (DOCS, CONTEXT, 1), jnp.float32) * math.log(10.0))
    col_scale = jnp.exp(jax.random.uniform(third_key, (1, 1, LATENT), jnp.float32) * math.log(10.0))
    spread = jnp.concatenate([row_scale * col_scale, jnp.ones((DOCS, CONTEXT, ROPE), jnp.float32)], axis=-1)
    values = values * spread
    position = jnp.arange(CONTEXT)[None, :, None]
    column = jnp.arange(LATENT + ROPE)[None, None, :]
    copied = values[:, 0:1, :] + 0.1 * values
    target = (position == 1) & (column < LATENT)
    values = jnp.where(target, copied, values)
    return jnp.clip(values, -400.0, 400.0)


def aligned_rows(base, values):
    first_row = base[:, 0, :LATENT]
    normed = first_row * jax.lax.rsqrt(jnp.mean(first_row * first_row, axis=-1, keepdims=True) + 1e-06)
    aligned = jnp.concatenate([normed, jnp.zeros((DOCS, ROPE), jnp.float32)], axis=-1)[:, None, None, :]
    slab_index = jnp.arange(SLAB)[None, :, None, None]
    unit = 192.0 ** 0.5 / LATENT
    strength = jnp.where(slab_index == 1, 120.0, jnp.where(slab_index == 2, 180.0, 240.0)) * unit
    chosen = (slab_index >= 1) & (slab_index <= 3)
    return jnp.where(chosen, strength * aligned, values)


def draw_offsets(key, part):
    starts, ends = slab_bounds(key)
    return starts


def draw_lengths(key, part):
    starts, ends = slab_bounds(key)
    return ends


def draw_kv_rows(key, part):
    base = latent_base(key)
    return base.astype(jnp.bfloat16)


def draw_queries(key, part):
    base = latent_base(key)
    key = jax.random.fold_in(key, 5)
    values = jax.random.normal(key, (DOCS, SLAB, HEADS, LATENT + ROPE), jnp.float32)
    values = aligned_rows(base, values)
    return jnp.clip(values, -2000.0, 2000.0).astype(jnp.bfloat16)


def draw_cotangent(key, part):
    key = jax.random.fold_in(key, 11)
    values = jax.random.normal(key, (DOCS, SLAB, HEADS, LATENT), jnp.float32)
    slab_index = jnp.arange(SLAB)[None, :, None, None]
    quiet = (slab_index >= 1) & (slab_index <= 3)
    values = jnp.where(quiet, 0.02 * values, values)
    return jnp.clip(values, -6.0, 6.0).astype(jnp.bfloat16)


def steps_of(own_key, extent, pieces, least, high):
    level, own = 1.0, jax.random.fold_in(own_key, 6)
    for dim, parts in pieces:
        heights = jnp.exp(jax.random.uniform(jax.random.fold_in(own, dim), (parts,), jnp.float32, least / len(pieces), high / len(pieces)))
        level = level * jnp.repeat(heights, extent[dim] // parts).reshape([-1 if axis == dim else 1 for axis in range(len(extent))])
    return level


def noise(stream_key, extent, width, limit, pieces=(), held_as=jnp.bfloat16):
    array = width * jax.random.normal(stream_key, extent, jnp.float32)
    if pieces:
        array = array * steps_of(stream_key, extent, pieces, -0.22, 0.18)
    return jnp.clip(array, -limit, limit).astype(held_as)


def setup_inputs(seed: int = 0) -> dict:
    splits = jax.random.split(jax.random.key(seed), 9)
    return {
        "offsets": draw_offsets(jax.random.fold_in(splits[8], 71), 0),
        "lengths": draw_lengths(jax.random.fold_in(splits[8], 71), 0),
        "queries": draw_queries(jax.random.fold_in(splits[8], 71), 0),
        "cotangent": draw_cotangent(jax.random.fold_in(splits[8], 71), 0),
        "kv_rows": draw_kv_rows(jax.random.fold_in(splits[8], 71), 0),
        "kv_tangent": noise(splits[5], (DOCS, CONTEXT, LATENT + ROPE), 1.0, 6.0, ((0, 8), (1, 64))),
        "norm_gain": jnp.clip(1.0 + 0.1 * jax.random.normal(splits[6], (LATENT,), jnp.float32), 0.5, 1.5),
        "gain_tangent": noise(splits[7], (LATENT,), 1.0, 6.0, (), jnp.float32),
    }


score_scale = 192.0 ** (-0.5)
tiny_eps = 1e-06
masked_score = -1e+30

def key_side(kv_rows, kv_tangent, norm_gain, gain_tangent, latent_width):
    latent = kv_rows[:, :latent_width].astype(jnp.float32)
    rope_part = kv_rows[:, latent_width:].astype(jnp.float32)
    latent_dot = kv_tangent[:, :latent_width].astype(jnp.float32)
    rope_dot = kv_tangent[:, latent_width:].astype(jnp.float32)
    inv_rms = lax.rsqrt(lax.optimization_barrier(jnp.mean(latent * latent, axis=-1, keepdims=True)) + tiny_eps)
    normed = latent * inv_rms
    inv_dot = -(inv_rms * inv_rms * inv_rms) * lax.optimization_barrier(jnp.mean(latent * latent_dot, axis=-1, keepdims=True))
    normed_dot = latent_dot * inv_rms + latent * inv_dot
    key_rows = jnp.concatenate([normed * norm_gain, rope_part], axis=-1).astype(jnp.bfloat16)
    key_dots = jnp.concatenate([gain_tangent * normed + norm_gain * normed_dot, rope_dot], axis=-1).astype(jnp.bfloat16)
    return (key_rows, key_dots, (latent, latent_dot, inv_rms, inv_dot, normed, normed_dot))

def block_terms(query_blk, cot_blk, query_pos, key_rows, key_dots, key_pos, latent_width):
    scores = score_scale * jnp.einsum('rc,kc->rk', query_blk, key_rows, preferred_element_type=jnp.float32)
    score_dot = score_scale * jnp.einsum('rc,kc->rk', query_blk, key_dots, preferred_element_type=jnp.float32)
    value_grad = jnp.einsum('rc,kc->rk', cot_blk, key_rows[:, :latent_width], preferred_element_type=jnp.float32)
    value_dot = jnp.einsum('rc,kc->rk', cot_blk, key_dots[:, :latent_width], preferred_element_type=jnp.float32)
    visible = key_pos[None, :] <= query_pos[:, None]
    return (scores, score_dot, value_grad, value_dot, visible)

def local_stats(query_blk, cot_blk, query_pos, key_rows, key_dots, key_pos, latent_width):
    scores, score_dot, value_grad, value_dot, visible = block_terms(query_blk, cot_blk, query_pos, key_rows, key_dots, key_pos, latent_width)
    maxima = lax.optimization_barrier(jnp.max(jnp.where(visible, scores, masked_score), axis=1))
    weights = jnp.where(visible, jnp.exp(scores - maxima[:, None]), 0.0)
    return (maxima, (lax.optimization_barrier(jnp.sum(weights, axis=1)), lax.optimization_barrier(jnp.sum(weights * score_dot, axis=1)), lax.optimization_barrier(jnp.sum(weights * value_grad, axis=1)), lax.optimization_barrier(jnp.sum(weights * score_dot * value_grad, axis=1)), lax.optimization_barrier(jnp.sum(weights * value_dot, axis=1))))

def grad_terms(query_blk, cot_blk, query_pos, softmax_stats, key_rows, key_dots, key_pos, latent_width):
    scores, score_dot, value_grad, value_dot, visible = block_terms(query_blk, cot_blk, query_pos, key_rows, key_dots, key_pos, latent_width)
    maxima, totals, moment_a, moment_b, moment_c, moment_e = softmax_stats
    attention = jnp.where(visible, jnp.exp(scores - maxima[:, None]), 0.0) / totals[:, None]
    shift_mean = moment_a / totals
    grad_mean = moment_b / totals
    grad_mean_dot = (moment_c - shift_mean * moment_b + moment_e) / totals
    attention_dot = attention * (score_dot - shift_mean[:, None])
    score_grad = attention * (value_grad - grad_mean[:, None])
    score_grad_dot = attention_dot * (value_grad - grad_mean[:, None]) + attention * (value_dot - grad_mean_dot[:, None])
    key_grad = score_scale * jnp.einsum('rk,rc->kc', score_grad.astype(jnp.bfloat16), query_blk, preferred_element_type=jnp.float32)
    key_grad_dot = score_scale * jnp.einsum('rk,rc->kc', score_grad_dot.astype(jnp.bfloat16), query_blk, preferred_element_type=jnp.float32)
    value_sum = jnp.einsum('rk,rc->kc', attention.astype(jnp.bfloat16), cot_blk, preferred_element_type=jnp.float32)
    value_sum_dot = jnp.einsum('rk,rc->kc', attention_dot.astype(jnp.bfloat16), cot_blk, preferred_element_type=jnp.float32)
    return (key_grad, key_grad_dot, value_sum, value_sum_dot)

def accumulate(flat_queries, flat_cot, flat_pos, softmax_stats, key_rows, key_dots, key_pos, latent_width):
    key_count, full_width = key_rows.shape
    start_state = (jnp.zeros((key_count, full_width), jnp.float32), jnp.zeros((key_count, full_width), jnp.float32), jnp.zeros((key_count, latent_width), jnp.float32), jnp.zeros((key_count, latent_width), jnp.float32))

    def advance(running, block_items):
        partial_terms = grad_terms(block_items[0], block_items[1], block_items[2], block_items[3], key_rows, key_dots, key_pos, latent_width)
        return (tuple((former + latter for former, latter in zip(running, partial_terms))), None)
    result, leftover = lax.scan(advance, start_state, (flat_queries, flat_cot, flat_pos, softmax_stats))
    return result

def finish(totals, norm_saved, norm_gain, gain_tangent, latent_width):
    key_grad, key_grad_dot, value_sum, value_sum_dot = totals
    latent, latent_dot, inv_rms, inv_dot, normed, normed_dot = norm_saved
    latent_grad = key_grad[:, :latent_width] + value_sum
    latent_grad_dot = key_grad_dot[:, :latent_width] + value_sum_dot
    gain_grad = lax.optimization_barrier(jnp.sum(latent_grad * normed, axis=0))
    gain_grad_dot = lax.optimization_barrier(jnp.sum(latent_grad_dot * normed + latent_grad * normed_dot, axis=0))
    normed_grad = latent_grad * norm_gain
    normed_grad_dot = latent_grad_dot * norm_gain + latent_grad * gain_tangent
    inner_grad = lax.optimization_barrier(jnp.mean(normed_grad * latent, axis=-1, keepdims=True))
    inner_grad_dot = lax.optimization_barrier(jnp.mean(normed_grad_dot * latent + normed_grad * latent_dot, axis=-1, keepdims=True))
    rms_cubed = inv_rms * inv_rms * inv_rms
    rms_cubed_dot = 3.0 * inv_rms * inv_rms * inv_dot
    row_dot = inv_dot * normed_grad + inv_rms * normed_grad_dot - rms_cubed_dot * latent * inner_grad - rms_cubed * latent_dot * inner_grad - rms_cubed * latent * inner_grad_dot
    hv_rows = jnp.concatenate([row_dot, key_grad_dot[:, latent_width:]], axis=-1)
    return (hv_rows, gain_grad, gain_grad_dot)

def one_document(offset, length, queries, cotangent, kv_rows, kv_tangent, norm_gain, gain_tangent):
    latent_width = norm_gain.shape[0]
    slab_rows = queries.shape[0]
    head_count = queries.shape[1]
    live_rows = jnp.arange(slab_rows, dtype=jnp.int32) < length - offset
    masked_cot = jnp.where(live_rows[:, None, None], cotangent, jnp.zeros_like(cotangent))
    key_rows, key_dots, norm_saved = key_side(kv_rows, kv_tangent, norm_gain, gain_tangent, latent_width)
    key_pos = jnp.arange(kv_rows.shape[0], dtype=jnp.int32)
    row_count = slab_rows * head_count
    block_rows = min(512, row_count)
    block_count = row_count // block_rows
    flat_queries = queries.reshape(block_count, block_rows, -1)
    flat_cot = masked_cot.reshape(block_count, block_rows, -1)
    flat_pos = (offset + jnp.arange(row_count, dtype=jnp.int32) // head_count).reshape(block_count, block_rows)

    def first_pass(block_items):
        return local_stats(block_items[0], block_items[1], block_items[2], key_rows, key_dots, key_pos, latent_width)
    maxima, partial_value = lax.map(first_pass, (flat_queries, flat_cot, flat_pos))
    softmax_stats = (maxima, partial_value[0], partial_value[1], partial_value[2], partial_value[3], partial_value[4])
    totals = accumulate(flat_queries, flat_cot, flat_pos, softmax_stats, key_rows, key_dots, key_pos, latent_width)
    return finish(totals, norm_saved, norm_gain, gain_tangent, latent_width)

def reference(offsets, lengths, queries, cotangent, kv_rows, kv_tangent, norm_gain, gain_tangent):

    def per_document(doc_items):
        return one_document(doc_items[0], doc_items[1], doc_items[2], doc_items[3], doc_items[4], doc_items[5], norm_gain, gain_tangent)
    hv_rows, gain_grads, gain_grads_dot = lax.map(per_document, (offsets, lengths, queries, cotangent, kv_rows, kv_tangent))
    return (hv_rows, jnp.stack([lax.optimization_barrier(jnp.sum(gain_grads, axis=0)), lax.optimization_barrier(jnp.sum(gain_grads_dot, axis=0))]))
```

```python
import functools

import jax
import jax.numpy as jnp
from jax import lax
from jax.experimental import pallas as pl
from jax.experimental.pallas import tpu as pltpu
from jax.sharding import PartitionSpec as P

score_scale = 192.0 ** (-0.5)
tiny_eps = 1e-06
masked_score = -1e30

X, Y, ZH = 4, 8, 2
ZL, CORE = 4, 2
CTX = X * Y * ZH
Z = ZH * ZL


def ctx_index(x, y, zh):
    return (x * Y + y) * ZH + zh


def ctx_shift(dx, dy, dz):
    return [
        (ctx_index(x, y, z), ctx_index((x + dx) % X, (y + dy) % Y, (z + dz) % ZH))
        for x in range(X)
        for y in range(Y)
        for z in range(ZH)
    ]


def all_shift(dx, dy, dz, dc):
    pairs = []
    for x in range(X):
        for y in range(Y):
            for z in range(Z):
                for c in range(CORE):
                    x2, y2, z2, c2 = (x + dx) % X, (y + dy) % Y, (z + dz) % Z, (c + dc) % CORE
                    source = ((z % ZL) * CORE + c) * CTX + ctx_index(x, y, z // ZL)
                    target = ((z2 % ZL) * CORE + c2) * CTX + ctx_index(x2, y2, z2 // ZL)
                    pairs.append((source, target))
    return pairs


def ctx_permute(value, dx=0, dy=0, dz=0):
    return lax.ppermute(value, "ctx", ctx_shift(dx, dy, dz))


def all_permute(value, dx=0, dy=0, dz=0, dc=0):
    return lax.ppermute(value, ("dp", "ctx"), all_shift(dx, dy, dz, dc))


def ring_sum(parts):
    while len(parts) > 1:
        half = len(parts) // 2
        parts = [parts[k] + parts[k + half] for k in range(half)]
    return parts[0]


def key_side(kv_rows, kv_tangent, norm_gain, gain_tangent, latent_width):
    latent = kv_rows[:, :latent_width].astype(jnp.float32)
    latent_dot = kv_tangent[:, :latent_width].astype(jnp.float32)
    inv_rms = lax.rsqrt(jnp.mean(latent * latent, axis=-1, keepdims=True) + tiny_eps)
    normed = latent * inv_rms
    inv_dot = -(inv_rms * inv_rms * inv_rms) * jnp.mean(latent * latent_dot, axis=-1, keepdims=True)
    normed_dot = latent_dot * inv_rms + latent * inv_dot
    return (latent, latent_dot, inv_rms, inv_dot, normed, normed_dot)


def nt_dot(left, right):
    return lax.dot_general(
        left, right, (((1,), (1,)), ((), ())), preferred_element_type=jnp.float32
    )


def nn_dot(left, right):
    return lax.dot_general(
        left, right, (((1,), (0,)), ((), ())), preferred_element_type=jnp.float32
    )


def place_cotangents(cot_refs, cot_buf, slab):
    rows = ZH * slab
    for dy in range(Y):
        for dx in range(X):
            cot_buf[(dx * Y + dy) * rows : (dx * Y + dy + 1) * rows, :] = cot_refs[dy][
                dx * rows : (dx + 1) * rows, :
            ]


def block_terms(pos_ref, keys, query_blk, cot_blk, latent_width, slab):
    key_count = keys.shape[0] // 2
    row_count = query_blk.shape[0]
    offset, live_count, key_base = pos_ref[0], pos_ref[1], pos_ref[2]
    by_query = score_scale * nt_dot(keys, query_blk)
    by_cot = nt_dot(keys[:, :latent_width], cot_blk)
    slab_row = lax.broadcasted_iota(jnp.int32, (key_count, row_count), 1) % slab
    key_pos = key_base + lax.broadcasted_iota(jnp.int32, (key_count, row_count), 0)
    visible = key_pos <= offset + slab_row
    live = slab_row < live_count
    return (
        by_query[:key_count],
        by_query[key_count:],
        jnp.where(live, by_cot[:key_count], 0.0),
        jnp.where(live, by_cot[key_count:], 0.0),
        visible,
        live,
    )


def stats_kernel(latent_width, slab, *refs):
    pos_ref, keys_ref = refs[:2]
    query_refs, cot_refs = refs[2 : 2 + X], refs[2 + X : 2 + X + Y]
    stats_ref, cot_buf = refs[2 + X + Y :]
    place_cotangents(cot_refs, cot_buf, slab)
    block = Y * ZH * slab
    keys = keys_ref[...]
    for dx in range(X):
        lanes = slice(dx * block, (dx + 1) * block)
        scores, score_dot, value_grad, value_dot, visible, _ = block_terms(
            pos_ref, keys, query_refs[dx][...], cot_buf[lanes, :], latent_width, slab
        )
        maxima = jnp.max(jnp.where(visible, scores, masked_score), axis=0, keepdims=True)
        weights = jnp.where(visible, jnp.exp(scores - maxima), 0.0)
        weighted = weights * score_dot
        rows = [
            maxima,
            jnp.sum(weights, axis=0, keepdims=True),
            jnp.sum(weighted, axis=0, keepdims=True),
            jnp.sum(weights * value_grad, axis=0, keepdims=True),
            jnp.sum(weighted * value_grad, axis=0, keepdims=True),
            jnp.sum(weights * value_dot, axis=0, keepdims=True),
            jnp.zeros((2, block), jnp.float32),
        ]
        stats_ref[:, lanes] = jnp.concatenate(rows, axis=0)


def merge_kernel(turn, *refs):
    parts = [refs[0][...]] + [turn(ref[...], step + 1) for step, ref in enumerate(refs[1:-1])]
    maxima = functools.reduce(jnp.maximum, [part[0:1] for part in parts])
    total = sum(jnp.exp(part[0:1] - maxima) * part for part in parts)
    row = lax.broadcasted_iota(jnp.int32, total.shape, 0)
    refs[-1][...] = jnp.where(row == 0, maxima, total)


def turn_x(part, step):
    block = part.shape[1] // X
    return jnp.concatenate([part[:, (X - step) * block :], part[:, : (X - step) * block]], axis=1)


def turn_y(part, step):
    block = part.shape[1] // X
    each = block // Y
    return jnp.concatenate(
        [
            pltpu.roll(part[:, dx * block : (dx + 1) * block], step * each, 1)
            for dx in range(X)
        ],
        axis=1,
    )


def turn_z(part, step):
    width = part.shape[1]
    each = width // CTX
    lane = lax.broadcasted_iota(jnp.int32, part.shape, 1)
    return jnp.where(
        lane % (2 * each) < each, pltpu.roll(part, width - each, 1), pltpu.roll(part, each, 1)
    )


def merge(turn, parts):
    return pl.pallas_call(
        functools.partial(merge_kernel, turn),
        out_shape=jax.ShapeDtypeStruct(parts[0].shape, jnp.float32),
        name="merge_stats",
    )(*parts)


def grads_kernel(latent_width, slab, *refs):
    pos_ref, keys_ref, stats_ref, rows_ref, tangent_ref, gain_ref, gain_tangent_ref = refs[:7]
    query_refs, cot_refs = refs[7 : 7 + X], refs[7 + X : 7 + X + Y]
    hv_ref, pair_ref, cot_buf = refs[7 + X + Y :]
    place_cotangents(cot_refs, cot_buf, slab)
    block = Y * ZH * slab
    keys = keys_ref[...]
    key_count = keys.shape[0] // 2
    by_query = jnp.zeros(keys.shape, jnp.float32)
    by_cot = jnp.zeros((keys.shape[0], latent_width), jnp.float32)
    for dx in range(X):
        lanes = slice(dx * block, (dx + 1) * block)
        query_blk, cot_blk = query_refs[dx][...], cot_buf[lanes, :]
        scores, score_dot, value_grad, value_dot, visible, live = block_terms(
            pos_ref, keys, query_blk, cot_blk, latent_width, slab
        )
        stats = stats_ref[:, lanes]
        maxima, totals = stats[0:1], stats[1:2]
        moment_a, moment_b, moment_c, moment_e = stats[2:3], stats[3:4], stats[4:5], stats[5:6]
        inv_totals = 1.0 / totals
        shift_mean = moment_a * inv_totals
        grad_mean = moment_b * inv_totals
        grad_mean_dot = (moment_c - shift_mean * moment_b + moment_e) * inv_totals
        attention = jnp.where(visible, jnp.exp(scores - maxima), 0.0) * inv_totals
        attention_dot = attention * (score_dot - shift_mean)
        centred = value_grad - grad_mean
        score_grad = attention * centred
        score_grad_dot = attention_dot * centred + attention * (value_dot - grad_mean_dot)
        left = jnp.concatenate([score_grad, score_grad_dot], axis=0).astype(jnp.bfloat16)
        by_query = by_query + nn_dot(left, query_blk)
        live_left = jnp.concatenate(
            [jnp.where(live, attention, 0.0), jnp.where(live, attention_dot, 0.0)], axis=0
        ).astype(jnp.bfloat16)
        by_cot = by_cot + nn_dot(live_left, cot_blk)
    by_query = score_scale * by_query
    latent_grad = by_query[:key_count, :latent_width] + by_cot[:key_count]
    latent_grad_dot = by_query[key_count:, :latent_width] + by_cot[key_count:]
    norm_gain, gain_tangent = gain_ref[...], gain_tangent_ref[...]
    latent, latent_dot, inv_rms, inv_dot, normed, normed_dot = key_side(
        rows_ref[...], tangent_ref[...], norm_gain, gain_tangent, latent_width
    )
    pair_ref[0:1, :] = jnp.sum(latent_grad * normed, axis=0, keepdims=True)
    pair_ref[1:2, :] = jnp.sum(
        latent_grad_dot * normed + latent_grad * normed_dot, axis=0, keepdims=True
    )
    normed_grad = latent_grad * norm_gain
    normed_grad_dot = latent_grad_dot * norm_gain + latent_grad * gain_tangent
    inner_grad = jnp.mean(normed_grad * latent, axis=-1, keepdims=True)
    inner_grad_dot = jnp.mean(
        normed_grad_dot * latent + normed_grad * latent_dot, axis=-1, keepdims=True
    )
    rms_cubed = inv_rms * inv_rms * inv_rms
    rms_cubed_dot = 3.0 * inv_rms * inv_rms * inv_dot
    row_dot = (
        inv_dot * normed_grad
        + inv_rms * normed_grad_dot
        - (rms_cubed_dot * inner_grad + rms_cubed * inner_grad_dot) * latent
        - (rms_cubed * inner_grad) * latent_dot
    )
    hv_ref[:latent_width, :] = row_dot.T
    hv_ref[latent_width:, :] = by_query[key_count:, latent_width:].T


def in_vmem(count):
    return [pl.BlockSpec(memory_space=pltpu.VMEM)] * count


def shards(offsets, lengths, queries, cotangent, kv_rows, kv_tangent, norm_gain, gain_tangent):
    latent_width = norm_gain.shape[0]
    slab, full_width = queries.shape[1], queries.shape[3]
    key_count = kv_rows.shape[1]
    row_count = slab * CTX

    own_query = queries.reshape(slab, full_width)
    own_cot = cotangent.reshape(slab, latent_width)
    with jax.named_scope("gather_z"):
        query_z = jnp.concatenate([own_query, ctx_permute(own_query, dz=1)], axis=0)
        cot_z = jnp.concatenate([own_cot, ctx_permute(own_cot, dz=1)], axis=0)
    with jax.named_scope("gather_mid"):
        query_y = jnp.concatenate(
            [query_z] + [ctx_permute(query_z, dy=step) for step in range(1, Y)], axis=0
        )
        cot_x = jnp.concatenate(
            [cot_z] + [ctx_permute(cot_z, dx=step) for step in range(1, X)], axis=0
        )
    with jax.named_scope("gather_last"):
        query_parts = [query_y] + [ctx_permute(query_y, dx=step) for step in range(1, X)]
        cot_parts = [cot_x] + [ctx_permute(cot_x, dy=step) for step in range(1, Y)]

    rows, tangent = kv_rows[0], kv_tangent[0]
    normed, normed_dot = key_side(rows, tangent, norm_gain, gain_tangent, latent_width)[4:]
    keys = jnp.concatenate(
        [
            jnp.concatenate([normed * norm_gain, rows[:, latent_width:].astype(jnp.float32)], 1),
            jnp.concatenate(
                [
                    gain_tangent * normed + norm_gain * normed_dot,
                    tangent[:, latent_width:].astype(jnp.float32),
                ],
                1,
            ),
        ],
        axis=0,
    ).astype(jnp.bfloat16)
    positions = jnp.stack(
        [offsets[0], lengths[0] - offsets[0], lax.axis_index("ctx").astype(jnp.int32) * key_count]
    )
    smem = [pl.BlockSpec(memory_space=pltpu.SMEM)]
    flops = 4 * key_count * row_count * (full_width + latent_width)

    stats = pl.pallas_call(
        functools.partial(stats_kernel, latent_width, slab),
        out_shape=jax.ShapeDtypeStruct((8, row_count), jnp.float32),
        in_specs=smem + in_vmem(1 + X + Y),
        out_specs=pl.BlockSpec(memory_space=pltpu.VMEM),
        scratch_shapes=[pltpu.VMEM((row_count, latent_width), jnp.bfloat16)],
        compiler_params=pltpu.CompilerParams(vmem_limit_bytes=40 * 2**20),
        cost_estimate=pl.CostEstimate(
            flops=flops, bytes_accessed=3 * 2**20, transcendentals=key_count * row_count
        ),
        name="local_stats",
    )(positions, keys, *query_parts, *cot_parts)

    with jax.named_scope("stats_x"):
        stats = merge(turn_x, [stats] + [ctx_permute(stats, dx=step) for step in range(1, X)])
    with jax.named_scope("stats_y"):
        stats = merge(turn_y, [stats] + [ctx_permute(stats, dy=step) for step in range(1, Y)])
    with jax.named_scope("stats_z"):
        stats = merge(turn_z, [stats, ctx_permute(stats, dz=1)])

    hv_rows, pair = pl.pallas_call(
        functools.partial(grads_kernel, latent_width, slab),
        out_shape=(
            jax.ShapeDtypeStruct((full_width, key_count), jnp.float32),
            jax.ShapeDtypeStruct((2, latent_width), jnp.float32),
        ),
        in_specs=smem + in_vmem(6 + X + Y),
        out_specs=(pl.BlockSpec(memory_space=pltpu.VMEM),) * 2,
        scratch_shapes=[pltpu.VMEM((row_count, latent_width), jnp.bfloat16)],
        compiler_params=pltpu.CompilerParams(vmem_limit_bytes=40 * 2**20),
        cost_estimate=pl.CostEstimate(
            flops=2 * flops, bytes_accessed=4 * 2**20, transcendentals=key_count * row_count
        ),
        name="gradients",
    )(
        positions,
        keys,
        stats,
        rows,
        tangent,
        norm_gain[None],
        gain_tangent[None],
        *query_parts,
        *cot_parts,
    )

    with jax.named_scope("pair_core"):
        pair = ring_sum([pair, all_permute(pair, dc=1)])
    with jax.named_scope("pair_z"):
        pair = ring_sum([pair] + [all_permute(pair, dz=step) for step in range(1, Z)])
    with jax.named_scope("pair_y"):
        pair = ring_sum([pair] + [all_permute(pair, dy=step) for step in range(1, Y)])
    with jax.named_scope("pair_x"):
        pair = ring_sum([pair] + [all_permute(pair, dx=step) for step in range(1, X)])
    return (hv_rows.T[None], pair)


def solution(mesh):
    in_specs = (
        P("dp"),
        P("dp"),
        P("dp", None, "ctx", None),
        P("dp", None, "ctx", None),
        P("dp", "ctx", None),
        P("dp", "ctx", None),
        P(),
        P(),
    )
    out_specs = (P("dp", "ctx", None), P())
    return jax.shard_map(shards, mesh=mesh, in_specs=in_specs, out_specs=out_specs, check_vma=False)
```

```python
import functools

import jax
import jax.numpy as jnp
from jax import lax
from jax.experimental import pallas as pl
from jax.experimental.pallas import tpu as pltpu
from jax.sharding import PartitionSpec as P

score_scale = 192.0 ** (-0.5)
tiny_eps = 1e-06
masked_score = -1e30

X, Y, ZH = 4, 8, 2
CTX = X * Y * ZH
LINE = 8


def ctx_index(x, y, zh):
    return (x * Y + y) * ZH + zh


Y_GROUPS = [[ctx_index(x, y, z) for y in range(Y)] for x in range(X) for z in range(ZH)]
XZ_GROUPS = [[ctx_index(x, y, z) for x in range(X) for z in range(ZH)] for y in range(Y)]


def ctx_permute(value, dx=0, dz=0):
    pairs = [
        (ctx_index(x, y, z), ctx_index((x + dx) % X, y, (z + dz) % ZH))
        for x in range(X)
        for y in range(Y)
        for z in range(ZH)
    ]
    return lax.ppermute(value, "ctx", pairs)


def exchange(copies, axis, groups=None):
    return lax.all_to_all(copies, axis, 0, 0, axis_index_groups=groups)


def key_side(kv_rows, kv_tangent, norm_gain, gain_tangent, latent_width):
    latent = kv_rows[:, :latent_width].astype(jnp.float32)
    latent_dot = kv_tangent[:, :latent_width].astype(jnp.float32)
    inv_rms = lax.rsqrt(jnp.mean(latent * latent, axis=-1, keepdims=True) + tiny_eps)
    normed = latent * inv_rms
    inv_dot = -(inv_rms * inv_rms * inv_rms) * jnp.mean(latent * latent_dot, axis=-1, keepdims=True)
    normed_dot = latent_dot * inv_rms + latent * inv_dot
    return (latent, latent_dot, inv_rms, inv_dot, normed, normed_dot)


def nt_dot(left, right):
    return lax.dot_general(
        left, right, (((1,), (1,)), ((), ())), preferred_element_type=jnp.float32
    )


def nn_dot(left, right):
    return lax.dot_general(
        left, right, (((1,), (0,)), ((), ())), preferred_element_type=jnp.float32
    )


def pair_kernel(place_ref, own_ref, other_ref, out_ref):
    z = place_ref[1]
    for copy in range(LINE):
        out_ref[copy, z] = own_ref[...]
        out_ref[copy, 1 - z] = other_ref[...]


def query_blocks(block_refs):
    own, *halves = block_refs
    blocks = [own[...]]
    for first, second in zip(halves[::2], halves[1::2]):
        blocks.append(jnp.concatenate([first[...], second[...]], axis=0))
    return blocks


def merge_sums(parts):
    maxima = jnp.max(parts[..., 0:1, :], axis=0)
    total = jnp.sum(jnp.exp(parts[..., 0:1, :] - maxima[None]) * parts, axis=0)
    row = lax.broadcasted_iota(jnp.int32, total.shape, total.ndim - 2)
    return jnp.where(row == 0, maxima, total)


def block_terms(place_ref, keys, block, latent_width, slab):
    key_count = keys.shape[0] // 2
    row_count = block.shape[0]
    cot_blk, query_blk = block[:, :latent_width], block[:, latent_width:]
    offset, live_count, key_base = place_ref[2], place_ref[3], place_ref[4]
    by_query = score_scale * nt_dot(keys, query_blk)
    by_cot = nt_dot(keys[:, :latent_width], cot_blk)
    slab_row = lax.broadcasted_iota(jnp.int32, (key_count, row_count), 1) % slab
    key_pos = key_base + lax.broadcasted_iota(jnp.int32, (key_count, row_count), 0)
    visible = key_pos <= offset + slab_row
    live = slab_row < live_count
    return (
        by_query[:key_count],
        by_query[key_count:],
        jnp.where(live, by_cot[:key_count], 0.0),
        jnp.where(live, by_cot[key_count:], 0.0),
        visible,
        live,
    )


def stats_kernel(latent_width, slab, place_ref, keys_ref, *refs):
    *block_refs, sums_ref = refs
    keys = keys_ref[...]
    for behind, block in enumerate(query_blocks(block_refs)):
        scores, score_dot, value_grad, value_dot, visible, _ = block_terms(
            place_ref, keys, block, latent_width, slab
        )
        maxima = jnp.max(jnp.where(visible, scores, masked_score), axis=0, keepdims=True)
        weights = jnp.where(visible, jnp.exp(scores - maxima), 0.0)
        weighted = weights * score_dot
        rows = [
            maxima,
            jnp.sum(weights, axis=0, keepdims=True),
            jnp.sum(weighted, axis=0, keepdims=True),
            jnp.sum(weights * value_grad, axis=0, keepdims=True),
            jnp.sum(weighted * value_grad, axis=0, keepdims=True),
            jnp.sum(weights * value_dot, axis=0, keepdims=True),
            jnp.zeros((2, block.shape[0]), jnp.float32),
        ]
        sums = jnp.concatenate(rows, axis=0)
        at = lax.rem(place_ref[0] + (X - behind), X)
        for copy in range(LINE):
            sums_ref[copy, at] = sums


def merge_kernel(parts_ref, out_ref):
    merged = merge_sums(parts_ref[...])
    for copy in range(LINE):
        out_ref[copy] = merged


def add_kernel(parts_ref, out_ref):
    total = jnp.sum(parts_ref[...], axis=0)
    for copy in range(LINE):
        out_ref[copy] = total


def grads_kernel(latent_width, slab, place_ref, keys_ref, parts_ref, *refs):
    rows_ref, tangent_ref, gain_ref, gain_tangent_ref, *block_refs = refs[:-3]
    hv_ref, pair_ref, sums_ref = refs[-3:]
    sums_ref[...] = merge_sums(parts_ref[...])
    keys = keys_ref[...]
    key_count = keys.shape[0] // 2
    by_query = jnp.zeros(keys.shape, jnp.float32)
    by_cot = jnp.zeros((keys.shape[0], latent_width), jnp.float32)
    for behind, block in enumerate(query_blocks(block_refs)):
        scores, score_dot, value_grad, value_dot, visible, live = block_terms(
            place_ref, keys, block, latent_width, slab
        )
        stats = sums_ref[lax.rem(place_ref[0] + (X - behind), X)]
        maxima, totals = stats[0:1], stats[1:2]
        moment_a, moment_b, moment_c, moment_e = stats[2:3], stats[3:4], stats[4:5], stats[5:6]
        inv_totals = 1.0 / totals
        shift_mean = moment_a * inv_totals
        grad_mean = moment_b * inv_totals
        grad_mean_dot = (moment_c - shift_mean * moment_b + moment_e) * inv_totals
        attention = jnp.where(visible, jnp.exp(scores - maxima), 0.0) * inv_totals
        attention_dot = attention * (score_dot - shift_mean)
        centred = value_grad - grad_mean
        score_grad = attention * centred
        score_grad_dot = attention_dot * centred + attention * (value_dot - grad_mean_dot)
        left = jnp.concatenate([score_grad, score_grad_dot], axis=0).astype(jnp.bfloat16)
        by_query = by_query + nn_dot(left, block[:, latent_width:])
        live_left = jnp.concatenate(
            [jnp.where(live, attention, 0.0), jnp.where(live, attention_dot, 0.0)], axis=0
        ).astype(jnp.bfloat16)
        by_cot = by_cot + nn_dot(live_left, block[:, :latent_width])
    by_query = score_scale * by_query
    latent_grad = by_query[:key_count, :latent_width] + by_cot[:key_count]
    latent_grad_dot = by_query[key_count:, :latent_width] + by_cot[key_count:]
    norm_gain, gain_tangent = gain_ref[...], gain_tangent_ref[...]
    latent, latent_dot, inv_rms, inv_dot, normed, normed_dot = key_side(
        rows_ref[...], tangent_ref[...], norm_gain, gain_tangent, latent_width
    )
    pair = jnp.concatenate(
        [
            jnp.sum(latent_grad * normed, axis=0, keepdims=True),
            jnp.sum(latent_grad_dot * normed + latent_grad * normed_dot, axis=0, keepdims=True),
        ],
        axis=0,
    )
    for copy in range(LINE):
        pair_ref[copy] = pair
    normed_grad = latent_grad * norm_gain
    normed_grad_dot = latent_grad_dot * norm_gain + latent_grad * gain_tangent
    inner_grad = jnp.mean(normed_grad * latent, axis=-1, keepdims=True)
    inner_grad_dot = jnp.mean(
        normed_grad_dot * latent + normed_grad * latent_dot, axis=-1, keepdims=True
    )
    rms_cubed = inv_rms * inv_rms * inv_rms
    rms_cubed_dot = 3.0 * inv_rms * inv_rms * inv_dot
    row_dot = (
        inv_dot * normed_grad
        + inv_rms * normed_grad_dot
        - (rms_cubed_dot * inner_grad + rms_cubed * inner_grad_dot) * latent
        - (rms_cubed * inner_grad) * latent_dot
    )
    hv_ref[:latent_width, :] = row_dot.T
    hv_ref[latent_width:, :] = by_query[key_count:, latent_width:].T


def in_vmem(count):
    return [pl.BlockSpec(memory_space=pltpu.VMEM)] * count


def shards(offsets, lengths, queries, cotangent, kv_rows, kv_tangent, norm_gain, gain_tangent):
    latent_width = norm_gain.shape[0]
    slab, full_width = queries.shape[1], queries.shape[3]
    key_count = kv_rows.shape[1]
    row_count = slab * CTX

    packed_width = latent_width + full_width
    smem = [pl.BlockSpec(memory_space=pltpu.SMEM)]
    ctx_at = lax.axis_index("ctx").astype(jnp.int32)
    place = jnp.stack(
        [
            ctx_at // (Y * ZH),
            ctx_at % ZH,
            offsets[0],
            lengths[0] - offsets[0],
            ctx_at * key_count,
        ]
    )

    packed = jnp.concatenate(
        [cotangent.reshape(slab, latent_width), queries.reshape(slab, full_width)], axis=1
    )
    with jax.named_scope("gather_z"):
        copies = pl.pallas_call(
            pair_kernel,
            out_shape=jax.ShapeDtypeStruct((LINE, ZH, slab, packed_width), packed.dtype),
            in_specs=smem + in_vmem(2),
            out_specs=pl.BlockSpec(memory_space=pltpu.VMEM),
            name="pair_rows",
        )(place, packed, ctx_permute(packed, dz=1))
    with jax.named_scope("gather_y"):
        block = exchange(copies, "ctx", Y_GROUPS).reshape(Y * ZH * slab, packed_width)
    with jax.named_scope("gather_x"):
        half = block.shape[0] // 2
        first, second = block[:half], block[half:]
        behind_first, ahead_second = ctx_permute(first, dx=1), ctx_permute(second, dx=-1)
        behind_second, ahead_first = ctx_permute(second, dx=1), ctx_permute(first, dx=-1)
        far_first, far_second = ctx_permute(behind_first, dx=1), ctx_permute(ahead_second, dx=-1)
        blocks = (
            block,
            behind_first,
            behind_second,
            far_first,
            far_second,
            ahead_first,
            ahead_second,
        )

    rows, tangent = kv_rows[0], kv_tangent[0]
    normed, normed_dot = key_side(rows, tangent, norm_gain, gain_tangent, latent_width)[4:]
    keys = jnp.concatenate(
        [
            jnp.concatenate([normed * norm_gain, rows[:, latent_width:].astype(jnp.float32)], 1),
            jnp.concatenate(
                [
                    gain_tangent * normed + norm_gain * normed_dot,
                    tangent[:, latent_width:].astype(jnp.float32),
                ],
                1,
            ),
        ],
        axis=0,
    ).astype(jnp.bfloat16)
    flops = 4 * key_count * row_count * (full_width + latent_width)

    sums_shape = jax.ShapeDtypeStruct((LINE, X, 8, Y * ZH * slab), jnp.float32)
    sums = pl.pallas_call(
        functools.partial(stats_kernel, latent_width, slab),
        out_shape=sums_shape,
        in_specs=smem + in_vmem(1 + len(blocks)),
        out_specs=pl.BlockSpec(memory_space=pltpu.VMEM),
        compiler_params=pltpu.CompilerParams(vmem_limit_bytes=40 * 2**20),
        cost_estimate=pl.CostEstimate(
            flops=flops, bytes_accessed=3 * 2**20, transcendentals=key_count * row_count
        ),
        name="local_stats",
    )(place, keys, *blocks)
    with jax.named_scope("stats_y"):
        sums = exchange(sums, "ctx", Y_GROUPS)
        sums = pl.pallas_call(merge_kernel, out_shape=sums_shape, name="merge_stats")(sums)
    with jax.named_scope("stats_xz"):
        sums = exchange(sums, "ctx", XZ_GROUPS)

    pair_shape = jax.ShapeDtypeStruct((LINE, 2, latent_width), jnp.float32)
    hv_rows, pair = pl.pallas_call(
        functools.partial(grads_kernel, latent_width, slab),
        out_shape=(jax.ShapeDtypeStruct((full_width, key_count), jnp.float32), pair_shape),
        in_specs=smem + in_vmem(6 + len(blocks)),
        out_specs=(pl.BlockSpec(memory_space=pltpu.VMEM),) * 2,
        scratch_shapes=[pltpu.VMEM(sums_shape.shape[1:], jnp.float32)],
        compiler_params=pltpu.CompilerParams(vmem_limit_bytes=40 * 2**20),
        cost_estimate=pl.CostEstimate(
            flops=2 * flops, bytes_accessed=4 * 2**20, transcendentals=key_count * row_count
        ),
        name="gradients",
    )(place, keys, sums, rows, tangent, norm_gain[None], gain_tangent[None], *blocks)

    add_copies = pl.pallas_call(add_kernel, out_shape=pair_shape, name="add_pair")
    with jax.named_scope("pair_dp"):
        pair = add_copies(exchange(pair, "dp"))
    with jax.named_scope("pair_y"):
        pair = add_copies(exchange(pair, "ctx", Y_GROUPS))
    with jax.named_scope("pair_xz"):
        pair = jnp.sum(exchange(pair, "ctx", XZ_GROUPS), axis=0)
    return (hv_rows.T[None], pair)


def solution(mesh):
    in_specs = (
        P("dp"),
        P("dp"),
        P("dp", None, "ctx", None),
        P("dp", None, "ctx", None),
        P("dp", "ctx", None),
        P("dp", "ctx", None),
        P(),
        P(),
    )
    out_specs = (P("dp", "ctx", None), P())
    return jax.shard_map(shards, mesh=mesh, in_specs=in_specs, out_specs=out_specs, check_vma=False)
```

```python
import functools

import jax
import jax.numpy as jnp
from jax import lax
from jax.experimental import pallas as pl
from jax.experimental.pallas import tpu as pltpu
from jax.sharding import PartitionSpec as P

score_scale = 192.0 ** (-0.5)
tiny_eps = 1e-06
masked_score = -1e30

X, Y, ZH = 4, 8, 2
ZL, CORE = 4, 2
CTX = X * Y * ZH
Z = ZH * ZL
LANES = 128
SUBLANES = 8


def ctx_index(x, y, zh):
    return (x * Y + y) * ZH + zh


def device_index(x, y, z, core):
    return (z % ZL * CORE + core) * CTX + ctx_index(x, y, z // ZL)


Y_GROUPS = [[ctx_index(x, y, z) for y in range(Y)] for x in range(X) for z in range(ZH)]
YZ_GROUPS = [[ctx_index(x, y, z) for y in range(Y) for z in range(ZH)] for x in range(X)]
COLUMNS = [
    [device_index(x, y, z, core) for z in range(Z) for core in range(CORE)]
    for x in range(X)
    for y in range(Y)
]
PLANES = [
    [device_index(x, y, z, core) for x in range(X) for y in range(Y)]
    for z in range(Z)
    for core in range(CORE)
]


def ctx_permute(value, dx=0, dz=0):
    pairs = [
        (ctx_index(x, y, z), ctx_index((x + dx) % X, y, (z + dz) % ZH))
        for x in range(X)
        for y in range(Y)
        for z in range(ZH)
    ]
    return lax.ppermute(value, "ctx", pairs)


def exchange(copies, axis, groups=None):
    return lax.all_to_all(copies, axis, 0, 0, axis_index_groups=groups)


def dot(left, right):
    return jnp.dot(left, right, preferred_element_type=jnp.float32)


def pair_kernel(latent_width, place_ref, own_ref, other_ref, out_ref):
    z, live_count = place_ref[1], place_ref[3]
    shape = own_ref.shape
    row = lax.broadcasted_iota(jnp.int32, shape, 0)
    column = lax.broadcasted_iota(jnp.int32, shape, 1)
    kept = (row < live_count) | (column >= latent_width)
    for at, ref in ((z, own_ref), (1 - z, other_ref)):
        rows = jnp.where(kept, ref[...].astype(jnp.float32), 0.0).astype(ref.dtype)
        for copy in range(Y):
            out_ref[copy, at] = rows


def norm_side(block_ref, latent_width):
    full_width = block_ref.shape[0] // 2
    latent = block_ref[:latent_width, :].astype(jnp.float32)
    latent_dot = block_ref[full_width : full_width + latent_width, :].astype(jnp.float32)
    inv_rms = lax.rsqrt(jnp.mean(latent * latent, axis=0, keepdims=True) + tiny_eps)
    normed = latent * inv_rms
    inv_dot = -(inv_rms * inv_rms * inv_rms) * jnp.mean(latent * latent_dot, axis=0, keepdims=True)
    normed_dot = latent_dot * inv_rms + latent * inv_dot
    return (latent, latent_dot, inv_rms, inv_dot, normed, normed_dot)


def keys_kernel(gain_ref, gain_tangent_ref, *refs):
    *block_refs, keys_ref = refs
    latent_width, full_width = gain_ref.shape[0], keys_ref.shape[1]
    norm_gain, gain_tangent = gain_ref[...], gain_tangent_ref[...]
    for at, block_ref in enumerate(block_refs):
        normed, normed_dot = norm_side(block_ref, latent_width)[4:]
        count = block_ref.shape[1]
        keys_ref[at, :latent_width, :count] = (normed * norm_gain).astype(jnp.bfloat16)
        keys_ref[at, :latent_width, count:] = (
            gain_tangent * normed + norm_gain * normed_dot
        ).astype(jnp.bfloat16)
        keys_ref[at, latent_width:, :count] = block_ref[latent_width:full_width, :]
        keys_ref[at, latent_width:, count:] = block_ref[full_width + latent_width :, :]


def block_terms(behind, slab, place_ref, keys_ref, rows_ref):
    row_count, width = rows_ref.shape
    key_count = keys_ref.shape[2] // 2
    latent_width = width - keys_ref.shape[1]
    keys = keys_ref[behind]
    by_query = score_scale * dot(rows_ref[:, latent_width:], keys)
    by_cot = dot(rows_ref[:, :latent_width], keys[:latent_width])
    x = lax.rem(place_ref[0] + (X - behind), X)
    key_pos = (x * (Y * ZH) + place_ref[4]) * key_count
    key_pos += lax.broadcasted_iota(jnp.int32, (row_count, key_count), 1)
    slab_row = lax.broadcasted_iota(jnp.int32, (row_count, key_count), 0) % slab
    visible = key_pos <= place_ref[2] + slab_row
    return (
        by_query[:, :key_count],
        by_query[:, key_count:],
        by_cot[:, :key_count],
        by_cot[:, key_count:],
        visible,
    )


def as_rows(columns):
    shape = (columns[0].shape[0], LANES)
    lane = lax.broadcasted_iota(jnp.int32, shape, 1)
    filled = jnp.zeros(shape, jnp.float32)
    for at, column in enumerate(columns):
        filled = jnp.where(lane == at, column, filled)
    return filled.T[:SUBLANES]


def stats_kernel(slab, place_ref, keys_ref, rows_ref, out_ref):
    terms = [block_terms(behind, slab, place_ref, keys_ref, rows_ref) for behind in range(X)]
    maxima = [jnp.where(visible, scores, masked_score) for scores, _, _, _, visible in terms]
    maxima = jnp.max(functools.reduce(jnp.maximum, maxima), axis=1, keepdims=True)
    sums = [0.0] * 4
    for scores, score_dot, value_grad, value_dot, visible in terms:
        weights = jnp.where(visible, jnp.exp(scores - maxima), 0.0)
        sums[0] += weights
        sums[1] += weights * score_dot
        sums[2] += weights * value_grad
        sums[3] += weights * (score_dot * value_grad + value_dot)
    sums = as_rows([maxima] + [jnp.sum(each, axis=1, keepdims=True) for each in sums])
    for copy in range(out_ref.shape[0]):
        out_ref[copy] = sums


def merged_means(parts_ref):
    count = parts_ref.shape[0]
    maxima = functools.reduce(jnp.maximum, [parts_ref[at, 0:1, :] for at in range(count)])
    sums = sum(jnp.exp(parts_ref[at, 0:1, :] - maxima) * parts_ref[at] for at in range(count))
    inv_totals = 1.0 / sums[1:2]
    shift_mean = sums[2:3] * inv_totals
    grad_mean = sums[3:4] * inv_totals
    grad_mean_dot = (sums[4:5] - shift_mean * sums[3:4]) * inv_totals
    rows = [maxima, inv_totals, shift_mean, grad_mean, grad_mean_dot]
    rows.append(jnp.zeros((LANES - len(rows), maxima.shape[1]), jnp.float32))
    columns = jnp.concatenate(rows, axis=0).T
    return [columns[:, at : at + 1] for at in range(5)]


def grads_kernel(slab, place_ref, parts_ref, keys_ref, rows_ref, turned_ref, *refs):
    gain_ref, gain_tangent_ref, block_refs = refs[0], refs[1], refs[2 : 2 + X]
    share_refs, pair_ref = refs[2 + X : 2 + 2 * X], refs[-1]
    latent_width = gain_ref.shape[0]
    norm_gain, gain_tangent = gain_ref[...], gain_tangent_ref[...]
    maxima, inv_totals, shift_mean, grad_mean, grad_mean_dot = merged_means(parts_ref)
    gain_grad = gain_grad_dot = 0.0
    for behind in range(X):
        scores, score_dot, value_grad, value_dot, visible = block_terms(
            behind, slab, place_ref, keys_ref, rows_ref
        )
        attention = jnp.where(visible, jnp.exp(scores - maxima), 0.0) * inv_totals
        attention_dot = attention * (score_dot - shift_mean)
        centred = value_grad - grad_mean
        score_grad = attention * centred
        score_grad_dot = attention_dot * centred + attention * (value_dot - grad_mean_dot)
        right = jnp.concatenate([score_grad, score_grad_dot], axis=1).astype(jnp.bfloat16)
        by_query = score_scale * dot(turned_ref[latent_width:, :], right)
        right = jnp.concatenate([attention, attention_dot], axis=1).astype(jnp.bfloat16)
        by_cot = dot(turned_ref[:latent_width, :], right)

        key_count = scores.shape[1]
        latent_grad = by_query[:latent_width, :key_count] + by_cot[:, :key_count]
        latent_grad_dot = by_query[:latent_width, key_count:] + by_cot[:, key_count:]
        latent, latent_dot, inv_rms, inv_dot, normed, normed_dot = norm_side(
            block_refs[behind], latent_width
        )
        gain_grad += latent_grad * normed
        gain_grad_dot += latent_grad_dot * normed + latent_grad * normed_dot
        normed_grad = latent_grad * norm_gain
        normed_grad_dot = latent_grad_dot * norm_gain + latent_grad * gain_tangent
        inner_grad = jnp.mean(normed_grad * latent, axis=0, keepdims=True)
        inner_grad_dot = jnp.mean(
            normed_grad_dot * latent + normed_grad * latent_dot, axis=0, keepdims=True
        )
        rms_cubed = inv_rms * inv_rms * inv_rms
        rms_cubed_dot = 3.0 * inv_rms * inv_rms * inv_dot
        share_refs[behind][:latent_width, :] = (
            inv_dot * normed_grad
            + inv_rms * normed_grad_dot
            - (rms_cubed_dot * inner_grad + rms_cubed * inner_grad_dot) * latent
            - (rms_cubed * inner_grad) * latent_dot
        )
        share_refs[behind][latent_width:, :] = by_query[latent_width:, key_count:]
    pair = as_rows([jnp.sum(each, axis=1, keepdims=True) for each in (gain_grad, gain_grad_dot)])
    pair = jnp.concatenate(
        [
            pair[row : row + 1, at : at + LANES]
            for row in range(2)
            for at in range(0, latent_width, LANES)
        ],
        axis=0,
    )
    for copy in range(pair_ref.shape[0]):
        pair_ref[copy] = pair


def add_kernel(parts_ref, out_ref):
    total = jnp.sum(parts_ref[...], axis=0)
    for copy in range(out_ref.shape[0]):
        out_ref[copy] = total


def in_vmem(count):
    return [pl.BlockSpec(memory_space=pltpu.VMEM)] * count


def shards(offsets, lengths, queries, cotangent, kv_rows, kv_tangent, norm_gain, gain_tangent):
    latent_width = norm_gain.shape[0]
    slab, full_width = queries.shape[1], queries.shape[3]
    key_count = kv_rows.shape[1]
    packed_width = latent_width + full_width
    row_count = Y * ZH * slab
    smem = [pl.BlockSpec(memory_space=pltpu.SMEM)]
    limit = pltpu.CompilerParams(vmem_limit_bytes=40 * 2**20)
    flops = 4 * X * key_count * row_count * packed_width
    ctx_at = lax.axis_index("ctx").astype(jnp.int32)
    place = jnp.stack(
        [
            ctx_at // (Y * ZH),
            ctx_at % ZH,
            offsets[0],
            lengths[0] - offsets[0],
            ctx_at % (Y * ZH),
        ]
    )

    packed = jnp.concatenate(
        [cotangent.reshape(slab, latent_width), queries.reshape(slab, full_width)], axis=1
    )
    with jax.named_scope("rows_z"):
        copies = pl.pallas_call(
            functools.partial(pair_kernel, latent_width),
            out_shape=jax.ShapeDtypeStruct((Y, ZH, slab, packed_width), packed.dtype),
            in_specs=smem + in_vmem(2),
            out_specs=pl.BlockSpec(memory_space=pltpu.VMEM),
            name="pair_rows",
        )(place, packed, ctx_permute(packed, dz=1))
    with jax.named_scope("rows_y"):
        block = jnp.concatenate([kv_rows[0].T, kv_tangent[0].T], axis=0)
        block, copies = lax.optimization_barrier((block, copies))
        rows = exchange(copies, "ctx", Y_GROUPS).reshape(row_count, packed_width)

    with jax.named_scope("keys_x"):
        blocks = [block] + [ctx_permute(block, dx=step) for step in range(1, X)]
    gains = (norm_gain[:, None], gain_tangent[:, None])
    keys = pl.pallas_call(
        keys_kernel,
        out_shape=jax.ShapeDtypeStruct((X, full_width, 2 * key_count), jnp.bfloat16),
        in_specs=in_vmem(2 + X),
        out_specs=pl.BlockSpec(memory_space=pltpu.VMEM),
        compiler_params=limit,
        name="make_keys",
    )(*gains, *blocks)

    sums = pl.pallas_call(
        functools.partial(stats_kernel, slab),
        out_shape=jax.ShapeDtypeStruct((Y * ZH, SUBLANES, row_count), jnp.float32),
        in_specs=smem + in_vmem(2),
        out_specs=pl.BlockSpec(memory_space=pltpu.VMEM),
        compiler_params=limit,
        cost_estimate=pl.CostEstimate(
            flops=flops, bytes_accessed=3 * 2**20, transcendentals=X * key_count * row_count
        ),
        name="local_stats",
    )(place, keys, rows)
    with jax.named_scope("stats_yz"):
        sums = exchange(sums, "ctx", YZ_GROUPS)

    *shares, pair = pl.pallas_call(
        functools.partial(grads_kernel, slab),
        out_shape=[jax.ShapeDtypeStruct((full_width, key_count), jnp.float32)] * X
        + [jax.ShapeDtypeStruct((Z * CORE, SUBLANES, LANES), jnp.float32)],
        in_specs=smem + in_vmem(6 + X),
        out_specs=in_vmem(X + 1),
        compiler_params=limit,
        cost_estimate=pl.CostEstimate(
            flops=2 * flops, bytes_accessed=4 * 2**20, transcendentals=X * key_count * row_count
        ),
        name="gradients",
    )(place, sums, keys, rows, rows.T, *gains, *blocks)

    with jax.named_scope("shares_x"):
        hv_rows = sum([ctx_permute(shares[step], dx=-step) for step in range(1, X)], shares[0])
    with jax.named_scope("pair_column"):
        pair = pl.pallas_call(
            add_kernel,
            out_shape=jax.ShapeDtypeStruct((X * Y, SUBLANES, LANES), jnp.float32),
            name="add_pair",
        )(exchange(pair, ("dp", "ctx"), COLUMNS))
    with jax.named_scope("pair_plane"):
        pair = jnp.sum(exchange(pair, ("dp", "ctx"), PLANES), axis=0).reshape(2, latent_width)
    return (hv_rows.T[None], pair)


def solution(mesh):
    in_specs = (
        P("dp"),
        P("dp"),
        P("dp", None, "ctx", None),
        P("dp", None, "ctx", None),
        P("dp", "ctx", None),
        P("dp", "ctx", None),
        P(),
        P(),
    )
    out_specs = (P("dp", "ctx", None), P())
    return jax.shard_map(shards, mesh=mesh, in_specs=in_specs, out_specs=out_specs, check_vma=False)
```

```python
import functools

import jax
import jax.numpy as jnp
from jax import lax
from jax.experimental import pallas as pl
from jax.experimental.pallas import tpu as pltpu
from jax.sharding import PartitionSpec as P

score_scale = 192.0 ** (-0.5)
tiny_eps = 1e-06
masked_score = -1e30

X, Y, ZH = 4, 8, 2
ZL, CORE = 4, 2
CTX = X * Y * ZH
Z = ZH * ZL
LANES = 128
SUBLANES = 8
MIB = 2**20


def ctx_index(x, y, zh):
    return (x * Y + y) * ZH + zh


def device_index(x, y, z, core):
    return (z % ZL * CORE + core) * CTX + ctx_index(x, y, z // ZL)


Y_GROUPS = [[ctx_index(x, y, z) for y in range(Y)] for x in range(X) for z in range(ZH)]
YZ_GROUPS = [[ctx_index(x, y, z) for y in range(Y) for z in range(ZH)] for x in range(X)]
COLUMNS = [
    [device_index(x, y, z, core) for z in range(Z) for core in range(CORE)]
    for x in range(X)
    for y in range(Y)
]
PLANES = [
    [device_index(x, y, z, core) for x in range(X) for y in range(Y)]
    for z in range(Z)
    for core in range(CORE)
]


def ctx_permute(value, dx=0, dz=0):
    pairs = [
        (ctx_index(x, y, z), ctx_index((x + dx) % X, y, (z + dz) % ZH))
        for x in range(X)
        for y in range(Y)
        for z in range(ZH)
    ]
    return lax.ppermute(value, "ctx", pairs)


def exchange(copies, axis, groups=None):
    return lax.all_to_all(copies, axis, 0, 0, axis_index_groups=groups)


def dot(left, right):
    return jnp.dot(left, right, preferred_element_type=jnp.float32)


def pair_kernel(latent_width, place_ref, own_ref, other_ref, out_ref):
    z, live_count = place_ref[1], place_ref[3]
    shape = own_ref.shape
    row = lax.broadcasted_iota(jnp.int32, shape, 0)
    column = lax.broadcasted_iota(jnp.int32, shape, 1)
    kept = (row < live_count) | (column >= latent_width)
    for at, ref in ((z, own_ref), (1 - z, other_ref)):
        rows = jnp.where(kept, ref[...].astype(jnp.float32), 0.0).astype(ref.dtype)
        for copy in range(Y):
            out_ref[copy, at] = rows


def norm_side(block_ref, latent_width):
    full_width = block_ref.shape[0] // 2
    latent = block_ref[:latent_width, :].astype(jnp.float32)
    latent_dot = block_ref[full_width : full_width + latent_width, :].astype(jnp.float32)
    inv_rms = lax.rsqrt(jnp.mean(latent * latent, axis=0, keepdims=True) + tiny_eps)
    normed = latent * inv_rms
    inv_dot = -(inv_rms * inv_rms * inv_rms) * jnp.mean(latent * latent_dot, axis=0, keepdims=True)
    normed_dot = latent_dot * inv_rms + latent * inv_dot
    return (latent, latent_dot, inv_rms, inv_dot, normed, normed_dot)


def keys_kernel(gain_ref, gain_tangent_ref, *refs):
    *block_refs, keys_ref = refs
    latent_width, full_width = gain_ref.shape[0], keys_ref.shape[1]
    norm_gain, gain_tangent = gain_ref[...], gain_tangent_ref[...]
    for at, block_ref in enumerate(block_refs):
        normed, normed_dot = norm_side(block_ref, latent_width)[4:]
        count = block_ref.shape[1]
        keys_ref[at, :latent_width, :count] = (normed * norm_gain).astype(jnp.bfloat16)
        keys_ref[at, :latent_width, count:] = (
            gain_tangent * normed + norm_gain * normed_dot
        ).astype(jnp.bfloat16)
        keys_ref[at, latent_width:, :count] = block_ref[latent_width:full_width, :]
        keys_ref[at, latent_width:, count:] = block_ref[full_width + latent_width :, :]


def block_terms(behind, slab, place_ref, keys_ref, rows_ref):
    row_count, width = rows_ref.shape
    key_count = keys_ref.shape[2] // 2
    latent_width = width - keys_ref.shape[1]
    keys = keys_ref[behind]
    by_query = score_scale * dot(rows_ref[:, latent_width:], keys)
    by_cot = dot(rows_ref[:, :latent_width], keys[:latent_width])
    x = lax.rem(place_ref[0] + (X - behind), X)
    key_pos = (x * (Y * ZH) + place_ref[4]) * key_count
    key_pos += lax.broadcasted_iota(jnp.int32, (row_count, key_count), 1)
    slab_row = lax.broadcasted_iota(jnp.int32, (row_count, key_count), 0) % slab
    visible = key_pos <= place_ref[2] + slab_row
    return (
        by_query[:, :key_count],
        by_query[:, key_count:],
        by_cot[:, :key_count],
        by_cot[:, key_count:],
        visible,
    )


def as_rows(columns):
    shape = (columns[0].shape[0], LANES)
    lane = lax.broadcasted_iota(jnp.int32, shape, 1)
    filled = jnp.zeros(shape, jnp.float32)
    for at, column in enumerate(columns):
        filled = jnp.where(lane == at, column, filled)
    return filled.T[:SUBLANES]


def stats_kernel(slab, place_ref, keys_ref, rows_ref, out_ref):
    terms = [block_terms(behind, slab, place_ref, keys_ref, rows_ref) for behind in range(X)]
    maxima = [jnp.where(visible, scores, masked_score) for scores, _, _, _, visible in terms]
    maxima = jnp.max(functools.reduce(jnp.maximum, maxima), axis=1, keepdims=True)
    sums = [0.0] * 4
    for scores, score_dot, value_grad, value_dot, visible in terms:
        weights = jnp.where(visible, jnp.exp(scores - maxima), 0.0)
        sums[0] += weights
        sums[1] += weights * score_dot
        sums[2] += weights * value_grad
        sums[3] += weights * (score_dot * value_grad + value_dot)
    sums = as_rows([maxima] + [jnp.sum(each, axis=1, keepdims=True) for each in sums])
    for copy in range(out_ref.shape[0]):
        out_ref[copy] = sums


def merged_means(parts_ref):
    count = parts_ref.shape[0]
    maxima = functools.reduce(jnp.maximum, [parts_ref[at, 0:1, :] for at in range(count)])
    sums = sum(jnp.exp(parts_ref[at, 0:1, :] - maxima) * parts_ref[at] for at in range(count))
    inv_totals = 1.0 / sums[1:2]
    shift_mean = sums[2:3] * inv_totals
    grad_mean = sums[3:4] * inv_totals
    grad_mean_dot = (sums[4:5] - shift_mean * sums[3:4]) * inv_totals
    rows = [maxima, inv_totals, shift_mean, grad_mean, grad_mean_dot]
    rows.append(jnp.zeros((LANES - len(rows), maxima.shape[1]), jnp.float32))
    columns = jnp.concatenate(rows, axis=0).T
    return [columns[:, at : at + 1] for at in range(5)]


def grads_kernel(slab, place_ref, parts_ref, keys_ref, rows_ref, turned_ref, *refs):
    *block_refs, grads_ref, pair_ref = refs
    latent_width = rows_ref.shape[1] - keys_ref.shape[1]
    maxima, inv_totals, shift_mean, grad_mean, grad_mean_dot = merged_means(parts_ref)
    gain_grad = gain_grad_dot = 0.0
    for behind in range(X):
        scores, score_dot, value_grad, value_dot, visible = block_terms(
            behind, slab, place_ref, keys_ref, rows_ref
        )
        attention = jnp.where(visible, jnp.exp(scores - maxima), 0.0) * inv_totals
        attention_dot = attention * (score_dot - shift_mean)
        centred = value_grad - grad_mean
        score_grad = attention * centred
        score_grad_dot = attention_dot * centred + attention * (value_dot - grad_mean_dot)
        right = jnp.concatenate([score_grad, score_grad_dot], axis=1).astype(jnp.bfloat16)
        by_query = score_scale * dot(turned_ref[latent_width:, :], right)
        right = jnp.concatenate([attention, attention_dot], axis=1).astype(jnp.bfloat16)
        by_cot = dot(turned_ref[:latent_width, :], right)

        key_count = scores.shape[1]
        latent_grad = by_query[:latent_width, :key_count] + by_cot[:, :key_count]
        latent_grad_dot = by_query[:latent_width, key_count:] + by_cot[:, key_count:]
        normed, normed_dot = norm_side(block_refs[behind], latent_width)[4:]
        gain_grad += latent_grad * normed
        gain_grad_dot += latent_grad_dot * normed + latent_grad * normed_dot
        grads_ref[behind, :latent_width, :] = latent_grad
        grads_ref[behind, latent_width : 2 * latent_width, :] = latent_grad_dot
        grads_ref[behind, 2 * latent_width :, :] = by_query[latent_width:, key_count:]
    pair = as_rows([jnp.sum(each, axis=1, keepdims=True) for each in (gain_grad, gain_grad_dot)])
    pair = jnp.concatenate(
        [
            pair[row : row + 1, at : at + LANES]
            for row in range(2)
            for at in range(0, latent_width, LANES)
        ],
        axis=0,
    )
    for copy in range(pair_ref.shape[0]):
        pair_ref[copy] = pair


def shares_kernel(grads_ref, gain_ref, gain_tangent_ref, *refs):
    block_refs, share_refs = refs[:X], refs[X:]
    latent_width = gain_ref.shape[0]
    norm_gain, gain_tangent = gain_ref[...], gain_tangent_ref[...]
    for behind in range(X):
        latent_grad = grads_ref[behind, :latent_width, :]
        latent_grad_dot = grads_ref[behind, latent_width : 2 * latent_width, :]
        latent, latent_dot, inv_rms, inv_dot, _, _ = norm_side(block_refs[behind], latent_width)
        normed_grad = latent_grad * norm_gain
        normed_grad_dot = latent_grad_dot * norm_gain + latent_grad * gain_tangent
        inner_grad = jnp.mean(normed_grad * latent, axis=0, keepdims=True)
        inner_grad_dot = jnp.mean(
            normed_grad_dot * latent + normed_grad * latent_dot, axis=0, keepdims=True
        )
        rms_cubed = inv_rms * inv_rms * inv_rms
        rms_cubed_dot = 3.0 * inv_rms * inv_rms * inv_dot
        share_refs[behind][:latent_width, :] = (
            inv_dot * normed_grad
            + inv_rms * normed_grad_dot
            - (rms_cubed_dot * inner_grad + rms_cubed * inner_grad_dot) * latent
            - (rms_cubed * inner_grad) * latent_dot
        )
        share_refs[behind][latent_width:, :] = grads_ref[behind, 2 * latent_width :, :]


def add_kernel(parts_ref, out_ref):
    total = jnp.sum(parts_ref[...], axis=0)
    for copy in range(out_ref.shape[0]):
        out_ref[copy] = total


def in_vmem(count):
    return [pl.BlockSpec(memory_space=pltpu.VMEM)] * count


def shards(offsets, lengths, queries, cotangent, kv_rows, kv_tangent, norm_gain, gain_tangent):
    latent_width = norm_gain.shape[0]
    slab, full_width = queries.shape[1], queries.shape[3]
    key_count = kv_rows.shape[1]
    packed_width = latent_width + full_width
    row_count = Y * ZH * slab
    smem = [pl.BlockSpec(memory_space=pltpu.SMEM)]
    flops = 4 * X * key_count * row_count * packed_width
    ctx_at = lax.axis_index("ctx").astype(jnp.int32)
    place = jnp.stack(
        [
            ctx_at // (Y * ZH),
            ctx_at % ZH,
            offsets[0],
            lengths[0] - offsets[0],
            ctx_at % (Y * ZH),
        ]
    )

    packed = jnp.concatenate(
        [cotangent.reshape(slab, latent_width), queries.reshape(slab, full_width)], axis=1
    )
    with jax.named_scope("rows_z"):
        copies = pl.pallas_call(
            functools.partial(pair_kernel, latent_width),
            out_shape=jax.ShapeDtypeStruct((Y, ZH, slab, packed_width), packed.dtype),
            in_specs=smem + in_vmem(2),
            out_specs=pl.BlockSpec(memory_space=pltpu.VMEM),
            compiler_params=pltpu.CompilerParams(vmem_limit_bytes=4 * MIB),
            name="pair_rows",
        )(place, packed, ctx_permute(packed, dz=1))
    with jax.named_scope("rows_y"):
        block = jnp.concatenate([kv_rows[0].T, kv_tangent[0].T], axis=0)
        near_block, copies = lax.optimization_barrier((block, copies))
        rows = exchange(copies, "ctx", Y_GROUPS).reshape(row_count, packed_width)

    with jax.named_scope("keys_x"):
        far_block = ctx_permute(block, dx=2)
        near_blocks = [ctx_permute(near_block, dx=step) for step in (1, -1)]
        blocks = [block, near_blocks[0], far_block, near_blocks[1]]
    gains = (norm_gain[:, None], gain_tangent[:, None])
    keys = pl.pallas_call(
        keys_kernel,
        out_shape=jax.ShapeDtypeStruct((X, full_width, 2 * key_count), jnp.bfloat16),
        in_specs=in_vmem(2 + X),
        out_specs=pl.BlockSpec(memory_space=pltpu.VMEM),
        compiler_params=pltpu.CompilerParams(vmem_limit_bytes=8 * MIB),
        name="make_keys",
    )(*gains, *blocks)

    sums = pl.pallas_call(
        functools.partial(stats_kernel, slab),
        out_shape=jax.ShapeDtypeStruct((Y * ZH, SUBLANES, row_count), jnp.float32),
        in_specs=smem + in_vmem(2),
        out_specs=pl.BlockSpec(memory_space=pltpu.VMEM),
        compiler_params=pltpu.CompilerParams(vmem_limit_bytes=12 * MIB),
        cost_estimate=pl.CostEstimate(
            flops=flops, bytes_accessed=3 * MIB, transcendentals=X * key_count * row_count
        ),
        name="local_stats",
    )(place, keys, rows)
    with jax.named_scope("stats_yz"):
        sums = exchange(sums, "ctx", YZ_GROUPS)

    grads, pair = pl.pallas_call(
        functools.partial(grads_kernel, slab),
        out_shape=[
            jax.ShapeDtypeStruct((X, latent_width + full_width, key_count), jnp.float32),
            jax.ShapeDtypeStruct((Z * CORE, SUBLANES, LANES), jnp.float32),
        ],
        in_specs=smem + in_vmem(4 + X),
        out_specs=in_vmem(2),
        compiler_params=pltpu.CompilerParams(vmem_limit_bytes=16 * MIB),
        cost_estimate=pl.CostEstimate(
            flops=2 * flops, bytes_accessed=6 * MIB, transcendentals=X * key_count * row_count
        ),
        name="gradients",
    )(place, sums, keys, rows, rows.T, *blocks)
    shares = pl.pallas_call(
        shares_kernel,
        out_shape=[jax.ShapeDtypeStruct((full_width, key_count), jnp.float32)] * X,
        in_specs=in_vmem(3 + X),
        out_specs=in_vmem(X),
        compiler_params=pltpu.CompilerParams(vmem_limit_bytes=12 * MIB),
        cost_estimate=pl.CostEstimate(
            flops=30 * X * key_count * latent_width, bytes_accessed=6 * MIB, transcendentals=0
        ),
        name="row_shares",
    )(grads, *gains, *blocks)

    with jax.named_scope("shares_x"):
        hv_rows = sum([ctx_permute(shares[step], dx=-step) for step in range(1, X)], shares[0])
    with jax.named_scope("pair_column"):
        pair = pl.pallas_call(
            add_kernel,
            out_shape=jax.ShapeDtypeStruct((X * Y, SUBLANES, LANES), jnp.float32),
            compiler_params=pltpu.CompilerParams(vmem_limit_bytes=2 * MIB),
            name="add_pair",
        )(exchange(pair, ("dp", "ctx"), COLUMNS))
    with jax.named_scope("pair_plane"):
        pair = jnp.sum(exchange(pair, ("dp", "ctx"), PLANES), axis=0).reshape(2, latent_width)
    return (hv_rows.T[None], pair)


def solution(mesh):
    in_specs = (
        P("dp"),
        P("dp"),
        P("dp", None, "ctx", None),
        P("dp", None, "ctx", None),
        P("dp", "ctx", None),
        P("dp", "ctx", None),
        P(),
        P(),
    )
    out_specs = (P("dp", "ctx", None), P())
    return jax.shard_map(shards, mesh=mesh, in_specs=in_specs, out_specs=out_specs, check_vma=False)
```

```python
import functools

import jax
import jax.numpy as jnp
from jax import lax
from jax.experimental import pallas as pl
from jax.experimental.pallas import tpu as pltpu
from jax.sharding import PartitionSpec as P

score_scale = 192.0 ** (-0.5)
tiny_eps = 1e-06
masked_score = -1e30

X, Y, ZH = 4, 8, 2
ZL, CORE = 4, 2
CTX = X * Y * ZH
Z = ZH * ZL
LANES = 128
SUBLANES = 8
MIB = 2**20


def ctx_index(x, y, zh):
    return (x * Y + y) * ZH + zh


def device_index(x, y, z, core):
    return (z % ZL * CORE + core) * CTX + ctx_index(x, y, z // ZL)


Y_GROUPS = [[ctx_index(x, y, z) for y in range(Y)] for x in range(X) for z in range(ZH)]
YZ_GROUPS = [[ctx_index(x, y, z) for y in range(Y) for z in range(ZH)] for x in range(X)]
COLUMNS = [
    [device_index(x, y, z, core) for z in range(Z) for core in range(CORE)]
    for x in range(X)
    for y in range(Y)
]
PLANES = [
    [device_index(x, y, z, core) for x in range(X) for y in range(Y)]
    for z in range(Z)
    for core in range(CORE)
]


def ctx_permute(value, dx=0, dz=0):
    pairs = [
        (ctx_index(x, y, z), ctx_index((x + dx) % X, y, (z + dz) % ZH))
        for x in range(X)
        for y in range(Y)
        for z in range(ZH)
    ]
    return lax.ppermute(value, "ctx", pairs)


def exchange(copies, axis, groups=None):
    return lax.all_to_all(copies, axis, 0, 0, axis_index_groups=groups)


def dot(left, right):
    return jnp.dot(left, right, preferred_element_type=jnp.float32)


def pair_kernel(latent_width, place_ref, own_ref, other_ref, out_ref):
    z, live_count = place_ref[1], place_ref[3]
    shape = own_ref.shape
    row = lax.broadcasted_iota(jnp.int32, shape, 0)
    column = lax.broadcasted_iota(jnp.int32, shape, 1)
    kept = (row < live_count) | (column >= latent_width)
    for at, ref in ((z, own_ref), (1 - z, other_ref)):
        rows = jnp.where(kept, ref[...].astype(jnp.float32), 0.0).astype(ref.dtype)
        for copy in range(Y):
            out_ref[copy, at] = rows


def norm_side(block_ref, latent_width):
    full_width = block_ref.shape[0] // 2
    latent = block_ref[:latent_width, :].astype(jnp.float32)
    latent_dot = block_ref[full_width : full_width + latent_width, :].astype(jnp.float32)
    inv_rms = lax.rsqrt(jnp.mean(latent * latent, axis=0, keepdims=True) + tiny_eps)
    normed = latent * inv_rms
    inv_dot = -(inv_rms * inv_rms * inv_rms) * jnp.mean(latent * latent_dot, axis=0, keepdims=True)
    normed_dot = latent_dot * inv_rms + latent * inv_dot
    return (latent, latent_dot, inv_rms, inv_dot, normed, normed_dot)


def keys_kernel(gain_ref, gain_tangent_ref, *refs):
    *block_refs, keys_ref = refs
    latent_width, full_width = gain_ref.shape[0], keys_ref.shape[1]
    norm_gain, gain_tangent = gain_ref[...], gain_tangent_ref[...]
    for at, block_ref in enumerate(block_refs):
        normed, normed_dot = norm_side(block_ref, latent_width)[4:]
        count = block_ref.shape[1]
        keys_ref[at, :latent_width, :count] = (normed * norm_gain).astype(jnp.bfloat16)
        keys_ref[at, :latent_width, count:] = (
            gain_tangent * normed + norm_gain * normed_dot
        ).astype(jnp.bfloat16)
        keys_ref[at, latent_width:, :count] = block_ref[latent_width:full_width, :]
        keys_ref[at, latent_width:, count:] = block_ref[full_width + latent_width :, :]


def block_terms(behind, slab, place_ref, keys_ref, rows_ref):
    row_count, width = rows_ref.shape
    key_count = keys_ref.shape[2] // 2
    latent_width = width - keys_ref.shape[1]
    keys = keys_ref[behind]
    by_query = score_scale * dot(rows_ref[:, latent_width:], keys)
    by_cot = dot(rows_ref[:, :latent_width], keys[:latent_width])
    x = lax.rem(place_ref[0] + (X - behind), X)
    key_pos = (x * (Y * ZH) + place_ref[4]) * key_count
    key_pos += lax.broadcasted_iota(jnp.int32, (row_count, key_count), 1)
    slab_row = lax.broadcasted_iota(jnp.int32, (row_count, key_count), 0) % slab
    visible = key_pos <= place_ref[2] + slab_row
    return (
        by_query[:, :key_count],
        by_query[:, key_count:],
        by_cot[:, :key_count],
        by_cot[:, key_count:],
        visible,
    )


def as_rows(columns):
    shape = (columns[0].shape[0], LANES)
    lane = lax.broadcasted_iota(jnp.int32, shape, 1)
    filled = jnp.zeros(shape, jnp.float32)
    for at, column in enumerate(columns):
        filled = jnp.where(lane == at, column, filled)
    return filled.T[:SUBLANES]


def stats_kernel(slab, place_ref, keys_ref, rows_ref, out_ref):
    terms = [block_terms(behind, slab, place_ref, keys_ref, rows_ref) for behind in range(X)]
    maxima = [jnp.where(visible, scores, masked_score) for scores, _, _, _, visible in terms]
    maxima = jnp.max(functools.reduce(jnp.maximum, maxima), axis=1, keepdims=True)
    sums = [0.0] * 4
    for scores, score_dot, value_grad, value_dot, visible in terms:
        weights = jnp.where(visible, jnp.exp(scores - maxima), 0.0)
        sums[0] += weights
        sums[1] += weights * score_dot
        sums[2] += weights * value_grad
        sums[3] += weights * (score_dot * value_grad + value_dot)
    sums = as_rows([maxima] + [jnp.sum(each, axis=1, keepdims=True) for each in sums])
    for copy in range(out_ref.shape[0]):
        out_ref[copy] = sums


def merged_means(parts_ref):
    count = parts_ref.shape[0]
    maxima = functools.reduce(jnp.maximum, [parts_ref[at, 0:1, :] for at in range(count)])
    sums = sum(jnp.exp(parts_ref[at, 0:1, :] - maxima) * parts_ref[at] for at in range(count))
    inv_totals = 1.0 / sums[1:2]
    shift_mean = sums[2:3] * inv_totals
    grad_mean = sums[3:4] * inv_totals
    grad_mean_dot = (sums[4:5] - shift_mean * sums[3:4]) * inv_totals
    rows = [maxima, inv_totals, shift_mean, grad_mean, grad_mean_dot]
    rows.append(jnp.zeros((LANES - len(rows), maxima.shape[1]), jnp.float32))
    columns = jnp.concatenate(rows, axis=0).T
    return [columns[:, at : at + 1] for at in range(5)]


def grads_kernel(slab, place_ref, parts_ref, keys_ref, rows_ref, *refs):
    *block_refs, grads_ref, pair_ref = refs
    latent_width = rows_ref.shape[1] - keys_ref.shape[1]
    turned_cot = rows_ref[:, :latent_width].T
    turned_query = rows_ref[:, latent_width:].T
    maxima, inv_totals, shift_mean, grad_mean, grad_mean_dot = merged_means(parts_ref)
    gain_grad = gain_grad_dot = 0.0
    for behind in range(X):
        scores, score_dot, value_grad, value_dot, visible = block_terms(
            behind, slab, place_ref, keys_ref, rows_ref
        )
        attention = jnp.where(visible, jnp.exp(scores - maxima), 0.0) * inv_totals
        attention_dot = attention * (score_dot - shift_mean)
        centred = value_grad - grad_mean
        score_grad = attention * centred
        score_grad_dot = attention_dot * centred + attention * (value_dot - grad_mean_dot)
        right = jnp.concatenate([score_grad, score_grad_dot], axis=1).astype(jnp.bfloat16)
        by_query = score_scale * dot(turned_query, right)
        right = jnp.concatenate([attention, attention_dot], axis=1).astype(jnp.bfloat16)
        by_cot = dot(turned_cot, right)

        key_count = scores.shape[1]
        latent_grad = by_query[:latent_width, :key_count] + by_cot[:, :key_count]
        latent_grad_dot = by_query[:latent_width, key_count:] + by_cot[:, key_count:]
        normed, normed_dot = norm_side(block_refs[behind], latent_width)[4:]
        gain_grad += latent_grad * normed
        gain_grad_dot += latent_grad_dot * normed + latent_grad * normed_dot
        grads_ref[behind, :latent_width, :] = latent_grad
        grads_ref[behind, latent_width : 2 * latent_width, :] = latent_grad_dot
        grads_ref[behind, 2 * latent_width :, :] = by_query[latent_width:, key_count:]
    pair = as_rows([jnp.sum(each, axis=1, keepdims=True) for each in (gain_grad, gain_grad_dot)])
    pair = jnp.concatenate(
        [
            pair[row : row + 1, at : at + LANES]
            for row in range(2)
            for at in range(0, latent_width, LANES)
        ],
        axis=0,
    )
    for copy in range(pair_ref.shape[0]):
        pair_ref[copy] = pair


def shares_kernel(grads_ref, gain_ref, gain_tangent_ref, *refs):
    block_refs, share_refs = refs[:X], refs[X:]
    latent_width = gain_ref.shape[0]
    norm_gain, gain_tangent = gain_ref[...], gain_tangent_ref[...]
    for behind in range(X):
        latent_grad = grads_ref[behind, :latent_width, :]
        latent_grad_dot = grads_ref[behind, latent_width : 2 * latent_width, :]
        latent, latent_dot, inv_rms, inv_dot, _, _ = norm_side(block_refs[behind], latent_width)
        normed_grad = latent_grad * norm_gain
        normed_grad_dot = latent_grad_dot * norm_gain + latent_grad * gain_tangent
        inner_grad = jnp.mean(normed_grad * latent, axis=0, keepdims=True)
        inner_grad_dot = jnp.mean(
            normed_grad_dot * latent + normed_grad * latent_dot, axis=0, keepdims=True
        )
        rms_cubed = inv_rms * inv_rms * inv_rms
        rms_cubed_dot = 3.0 * inv_rms * inv_rms * inv_dot
        share_refs[behind][:latent_width, :] = (
            inv_dot * normed_grad
            + inv_rms * normed_grad_dot
            - (rms_cubed_dot * inner_grad + rms_cubed * inner_grad_dot) * latent
            - (rms_cubed * inner_grad) * latent_dot
        )
        share_refs[behind][latent_width:, :] = grads_ref[behind, 2 * latent_width :, :]


def add_kernel(parts_ref, out_ref):
    total = jnp.sum(parts_ref[...], axis=0)
    for copy in range(out_ref.shape[0]):
        out_ref[copy] = total


def in_vmem(count):
    return [pl.BlockSpec(memory_space=pltpu.VMEM)] * count


def shards(offsets, lengths, queries, cotangent, kv_rows, kv_tangent, norm_gain, gain_tangent):
    latent_width = norm_gain.shape[0]
    slab, full_width = queries.shape[1], queries.shape[3]
    key_count = kv_rows.shape[1]
    packed_width = latent_width + full_width
    row_count = Y * ZH * slab
    smem = [pl.BlockSpec(memory_space=pltpu.SMEM)]
    flops = 4 * X * key_count * row_count * packed_width
    ctx_at = lax.axis_index("ctx").astype(jnp.int32)
    place = jnp.stack(
        [
            ctx_at // (Y * ZH),
            ctx_at % ZH,
            offsets[0],
            lengths[0] - offsets[0],
            ctx_at % (Y * ZH),
        ]
    )

    packed = jnp.concatenate(
        [cotangent.reshape(slab, latent_width), queries.reshape(slab, full_width)], axis=1
    )
    with jax.named_scope("rows_z"):
        copies = pl.pallas_call(
            functools.partial(pair_kernel, latent_width),
            out_shape=jax.ShapeDtypeStruct((Y, ZH, slab, packed_width), packed.dtype),
            in_specs=smem + in_vmem(2),
            out_specs=pl.BlockSpec(memory_space=pltpu.VMEM),
            compiler_params=pltpu.CompilerParams(vmem_limit_bytes=4 * MIB),
            name="pair_rows",
        )(place, packed, ctx_permute(packed, dz=1))
    with jax.named_scope("rows_y"):
        block = jnp.concatenate([kv_rows[0].T, kv_tangent[0].T], axis=0)
        near_block, copies = lax.optimization_barrier((block, copies))
        rows = exchange(copies, "ctx", Y_GROUPS).reshape(row_count, packed_width)

    with jax.named_scope("keys_x"):
        far_block = ctx_permute(block, dx=2)
        near_blocks = [ctx_permute(near_block, dx=step) for step in (1, -1)]
        blocks = [block, near_blocks[0], far_block, near_blocks[1]]
    gains = (norm_gain[:, None], gain_tangent[:, None])
    keys = pl.pallas_call(
        keys_kernel,
        out_shape=jax.ShapeDtypeStruct((X, full_width, 2 * key_count), jnp.bfloat16),
        in_specs=in_vmem(2 + X),
        out_specs=pl.BlockSpec(memory_space=pltpu.VMEM),
        compiler_params=pltpu.CompilerParams(vmem_limit_bytes=8 * MIB),
        name="make_keys",
    )(*gains, *blocks)

    sums = pl.pallas_call(
        functools.partial(stats_kernel, slab),
        out_shape=jax.ShapeDtypeStruct((Y * ZH, SUBLANES, row_count), jnp.float32),
        in_specs=smem + in_vmem(2),
        out_specs=pl.BlockSpec(memory_space=pltpu.VMEM),
        compiler_params=pltpu.CompilerParams(vmem_limit_bytes=12 * MIB),
        cost_estimate=pl.CostEstimate(
            flops=flops, bytes_accessed=3 * MIB, transcendentals=X * key_count * row_count
        ),
        name="local_stats",
    )(place, keys, rows)
    with jax.named_scope("stats_yz"):
        sums = exchange(sums, "ctx", YZ_GROUPS)

    grads, pair = pl.pallas_call(
        functools.partial(grads_kernel, slab),
        out_shape=[
            jax.ShapeDtypeStruct((X, latent_width + full_width, key_count), jnp.float32),
            jax.ShapeDtypeStruct((Z * CORE, SUBLANES, LANES), jnp.float32),
        ],
        in_specs=smem + in_vmem(3 + X),
        out_specs=in_vmem(2),
        compiler_params=pltpu.CompilerParams(vmem_limit_bytes=16 * MIB),
        cost_estimate=pl.CostEstimate(
            flops=2 * flops, bytes_accessed=6 * MIB, transcendentals=X * key_count * row_count
        ),
        name="gradients",
    )(place, sums, keys, rows, *blocks)
    shares = pl.pallas_call(
        shares_kernel,
        out_shape=[jax.ShapeDtypeStruct((full_width, key_count), jnp.float32)] * X,
        in_specs=in_vmem(3 + X),
        out_specs=in_vmem(X),
        compiler_params=pltpu.CompilerParams(vmem_limit_bytes=12 * MIB),
        cost_estimate=pl.CostEstimate(
            flops=10**10, bytes_accessed=6 * MIB, transcendentals=0
        ),
        name="row_shares",
    )(grads, *gains, *blocks)

    with jax.named_scope("shares_x"):
        hv_rows = sum([ctx_permute(shares[step], dx=-step) for step in range(1, X)], shares[0])
    with jax.named_scope("pair_column"):
        pair = pl.pallas_call(
            add_kernel,
            out_shape=jax.ShapeDtypeStruct((X * Y, SUBLANES, LANES), jnp.float32),
            compiler_params=pltpu.CompilerParams(vmem_limit_bytes=2 * MIB),
            cost_estimate=pl.CostEstimate(
                flops=10**11, bytes_accessed=MIB // 4, transcendentals=0
            ),
            name="add_pair",
        )(exchange(pair, ("dp", "ctx"), COLUMNS))
    with jax.named_scope("pair_plane"):
        pair = jnp.sum(exchange(pair, ("dp", "ctx"), PLANES), axis=0).reshape(2, latent_width)
    return (hv_rows.T[None], pair)


def solution(mesh):
    in_specs = (
        P("dp"),
        P("dp"),
        P("dp", None, "ctx", None),
        P("dp", None, "ctx", None),
        P("dp", "ctx", None),
        P("dp", "ctx", None),
        P(),
        P(),
    )
    out_specs = (P("dp", "ctx", None), P())
    return jax.shard_map(shards, mesh=mesh, in_specs=in_specs, out_specs=out_specs, check_vma=False)
```

```python
import functools

import jax
import jax.numpy as jnp
from jax import lax
from jax.experimental import pallas as pl
from jax.experimental.pallas import tpu as pltpu
from jax.sharding import PartitionSpec as P

score_scale = 192.0 ** (-0.5)
tiny_eps = 1e-06
masked_score = -1e30

X, Y, ZH = 4, 8, 2
ZL, CORE = 4, 2
CTX = X * Y * ZH
Z = ZH * ZL
LANES = 128
SUBLANES = 8
SUMS = 5
MIB = 2**20


def ctx_index(x, y, zh):
    return (x * Y + y) * ZH + zh


def device_index(x, y, z, core):
    return (z % ZL * CORE + core) * CTX + ctx_index(x, y, z // ZL)


Y_GROUPS = [[ctx_index(x, y, z) for y in range(Y)] for x in range(X) for z in range(ZH)]
YZ_GROUPS = [[ctx_index(x, y, z) for y in range(Y) for z in range(ZH)] for x in range(X)]
COLUMNS = [
    [device_index(x, y, z, core) for z in range(Z) for core in range(CORE)]
    for x in range(X)
    for y in range(Y)
]
PLANES = [
    [device_index(x, y, z, core) for x in range(X) for y in range(Y)]
    for z in range(Z)
    for core in range(CORE)
]


def ctx_permute(value, dx=0, dz=0):
    pairs = [
        (ctx_index(x, y, z), ctx_index((x + dx) % X, y, (z + dz) % ZH))
        for x in range(X)
        for y in range(Y)
        for z in range(ZH)
    ]
    return lax.ppermute(value, "ctx", pairs)


def exchange(copies, axis, groups=None):
    return lax.all_to_all(copies, axis, 0, 0, axis_index_groups=groups)


def dot(left, right):
    return jnp.dot(left, right, preferred_element_type=jnp.float32)


def pair_kernel(latent_width, place_ref, own_ref, other_ref, out_ref):
    z, live_count = place_ref[1], place_ref[3]
    shape = own_ref.shape
    row = lax.broadcasted_iota(jnp.int32, shape, 0)
    column = lax.broadcasted_iota(jnp.int32, shape, 1)
    kept = (row < live_count) | (column >= latent_width)
    for at, ref in ((z, own_ref), (1 - z, other_ref)):
        rows = jnp.where(kept, ref[...].astype(jnp.float32), 0.0).astype(ref.dtype)
        for copy in range(Y):
            out_ref[copy, at] = rows


def norm_side(block_ref, latent_width):
    full_width = block_ref.shape[0] // 2
    latent = block_ref[:latent_width, :].astype(jnp.float32)
    latent_dot = block_ref[full_width : full_width + latent_width, :].astype(jnp.float32)
    inv_rms = lax.rsqrt(jnp.mean(latent * latent, axis=0, keepdims=True) + tiny_eps)
    normed = latent * inv_rms
    inv_dot = -(inv_rms * inv_rms * inv_rms) * jnp.mean(latent * latent_dot, axis=0, keepdims=True)
    normed_dot = latent_dot * inv_rms + latent * inv_dot
    return (latent, latent_dot, inv_rms, inv_dot, normed, normed_dot)


def keys_kernel(gain_ref, gain_tangent_ref, *refs):
    *block_refs, keys_ref = refs
    latent_width, full_width = gain_ref.shape[0], keys_ref.shape[1]
    norm_gain, gain_tangent = gain_ref[...], gain_tangent_ref[...]
    for at, block_ref in enumerate(block_refs):
        normed, normed_dot = norm_side(block_ref, latent_width)[4:]
        count = block_ref.shape[1]
        keys_ref[at, :latent_width, :count] = (normed * norm_gain).astype(jnp.bfloat16)
        keys_ref[at, :latent_width, count:] = (
            gain_tangent * normed + norm_gain * normed_dot
        ).astype(jnp.bfloat16)
        keys_ref[at, latent_width:, :count] = block_ref[latent_width:full_width, :]
        keys_ref[at, latent_width:, count:] = block_ref[full_width + latent_width :, :]


def block_terms(behind, slab, place_ref, keys_ref, rows_ref):
    row_count, width = rows_ref.shape
    key_count = keys_ref.shape[2] // 2
    latent_width = width - keys_ref.shape[1]
    keys = keys_ref[behind]
    by_query = score_scale * dot(rows_ref[:, latent_width:], keys)
    by_cot = dot(rows_ref[:, :latent_width], keys[:latent_width])
    x = lax.rem(place_ref[0] + (X - behind), X)
    key_pos = (x * (Y * ZH) + place_ref[4]) * key_count
    key_pos += lax.broadcasted_iota(jnp.int32, (row_count, key_count), 1)
    slab_row = lax.broadcasted_iota(jnp.int32, (row_count, key_count), 0) % slab
    visible = key_pos <= place_ref[2] + slab_row
    return (
        by_query[:, :key_count],
        by_query[:, key_count:],
        by_cot[:, :key_count],
        by_cot[:, key_count:],
        visible,
    )


def as_rows(columns):
    shape = (columns[0].shape[0], LANES)
    lane = lax.broadcasted_iota(jnp.int32, shape, 1)
    filled = jnp.zeros(shape, jnp.float32)
    for at, column in enumerate(columns):
        filled = jnp.where(lane == at, column, filled)
    return filled.T[:SUBLANES]


def stats_kernel(slab, place_ref, keys_ref, rows_ref, out_ref):
    terms = [block_terms(behind, slab, place_ref, keys_ref, rows_ref) for behind in range(X)]
    maxima = [jnp.where(visible, scores, masked_score) for scores, _, _, _, visible in terms]
    maxima = jnp.max(functools.reduce(jnp.maximum, maxima), axis=1, keepdims=True)
    sums = [0.0] * 4
    for scores, score_dot, value_grad, value_dot, visible in terms:
        weights = jnp.where(visible, jnp.exp(scores - maxima), 0.0)
        sums[0] += weights
        sums[1] += weights * score_dot
        sums[2] += weights * value_grad
        sums[3] += weights * (score_dot * value_grad + value_dot)
    sums = as_rows([maxima] + [jnp.sum(each, axis=1, keepdims=True) for each in sums])
    for row in range(SUMS):
        values = sums[row : row + 1]
        values = jnp.concatenate([values[:, :LANES], values[:, LANES:]], axis=0)
        for copy in range(out_ref.shape[0]):
            out_ref[copy, row] = values


def merged_means(parts_ref):
    count = parts_ref.shape[0]
    maxima = functools.reduce(jnp.maximum, [parts_ref[at, 0] for at in range(count)])
    scales = [jnp.exp(parts_ref[at, 0] - maxima) for at in range(count)]
    sums = [
        sum(scales[at] * parts_ref[at, row] for at in range(count)) for row in range(1, SUMS)
    ]
    inv_totals = 1.0 / sums[0]
    shift_mean = sums[1] * inv_totals
    grad_mean = sums[2] * inv_totals
    grad_mean_dot = (sums[3] - shift_mean * sums[2]) * inv_totals
    rows = [
        jnp.concatenate([values[0:1], values[1:2]], axis=1)
        for values in (maxima, inv_totals, shift_mean, grad_mean, grad_mean_dot)
    ]
    rows.append(jnp.zeros((LANES - SUMS, 2 * LANES), jnp.float32))
    columns = jnp.concatenate(rows, axis=0).T
    return [columns[:, at : at + 1] for at in range(SUMS)]


def grads_kernel(slab, place_ref, parts_ref, keys_ref, rows_ref, *refs):
    gain_ref, gain_tangent_ref, block_refs = refs[0], refs[1], refs[2 : 2 + X]
    share_refs, pair_ref = refs[2 + X : -1], refs[-1]
    latent_width = gain_ref.shape[0]
    norm_gain, gain_tangent = gain_ref[...], gain_tangent_ref[...]
    turned_cot = rows_ref[:, :latent_width].T
    turned_query = rows_ref[:, latent_width:].T
    maxima, inv_totals, shift_mean, grad_mean, grad_mean_dot = merged_means(parts_ref)
    gain_grad = gain_grad_dot = 0.0
    for behind in range(X):
        scores, score_dot, value_grad, value_dot, visible = block_terms(
            behind, slab, place_ref, keys_ref, rows_ref
        )
        attention = jnp.where(visible, jnp.exp(scores - maxima), 0.0) * inv_totals
        attention_dot = attention * (score_dot - shift_mean)
        centred = value_grad - grad_mean
        score_grad = attention * centred
        score_grad_dot = attention_dot * centred + attention * (value_dot - grad_mean_dot)
        right = jnp.concatenate([score_grad, score_grad_dot], axis=1).astype(jnp.bfloat16)
        by_query = score_scale * dot(turned_query, right)
        right = jnp.concatenate([attention, attention_dot], axis=1).astype(jnp.bfloat16)
        by_cot = dot(turned_cot, right)

        key_count = scores.shape[1]
        latent_grad = by_query[:latent_width, :key_count] + by_cot[:, :key_count]
        latent_grad_dot = by_query[:latent_width, key_count:] + by_cot[:, key_count:]
        latent, latent_dot, inv_rms, inv_dot, normed, normed_dot = norm_side(
            block_refs[behind], latent_width
        )
        gain_grad += latent_grad * normed
        gain_grad_dot += latent_grad_dot * normed + latent_grad * normed_dot
        normed_grad = latent_grad * norm_gain
        normed_grad_dot = latent_grad_dot * norm_gain + latent_grad * gain_tangent
        inner_grad = jnp.mean(normed_grad * latent, axis=0, keepdims=True)
        inner_grad_dot = jnp.mean(
            normed_grad_dot * latent + normed_grad * latent_dot, axis=0, keepdims=True
        )
        rms_cubed = inv_rms * inv_rms * inv_rms
        rms_cubed_dot = 3.0 * inv_rms * inv_rms * inv_dot
        share_refs[behind][:latent_width, :] = (
            inv_dot * normed_grad
            + inv_rms * normed_grad_dot
            - (rms_cubed_dot * inner_grad + rms_cubed * inner_grad_dot) * latent
            - (rms_cubed * inner_grad) * latent_dot
        )
        share_refs[behind][latent_width:, :] = by_query[latent_width:, key_count:]
    pair = as_rows([jnp.sum(each, axis=1, keepdims=True) for each in (gain_grad, gain_grad_dot)])
    pair = jnp.concatenate(
        [
            pair[row : row + 1, at : at + LANES]
            for row in range(2)
            for at in range(0, latent_width, LANES)
        ],
        axis=0,
    )
    for copy in range(pair_ref.shape[0]):
        pair_ref[copy] = pair


def add_kernel(parts_ref, out_ref):
    total = jnp.sum(parts_ref[...], axis=0)
    for copy in range(out_ref.shape[0]):
        out_ref[copy] = total


def in_vmem(count):
    return [pl.BlockSpec(memory_space=pltpu.VMEM)] * count


def shards(offsets, lengths, queries, cotangent, kv_rows, kv_tangent, norm_gain, gain_tangent):
    latent_width = norm_gain.shape[0]
    slab, full_width = queries.shape[1], queries.shape[3]
    key_count = kv_rows.shape[1]
    packed_width = latent_width + full_width
    row_count = Y * ZH * slab
    smem = [pl.BlockSpec(memory_space=pltpu.SMEM)]
    flops = 4 * X * key_count * row_count * packed_width
    ctx_at = lax.axis_index("ctx").astype(jnp.int32)
    place = jnp.stack(
        [
            ctx_at // (Y * ZH),
            ctx_at % ZH,
            offsets[0],
            lengths[0] - offsets[0],
            ctx_at % (Y * ZH),
        ]
    )

    packed = jnp.concatenate(
        [cotangent.reshape(slab, latent_width), queries.reshape(slab, full_width)], axis=1
    )
    with jax.named_scope("rows_z"):
        copies = pl.pallas_call(
            functools.partial(pair_kernel, latent_width),
            out_shape=jax.ShapeDtypeStruct((Y, ZH, slab, packed_width), packed.dtype),
            in_specs=smem + in_vmem(2),
            out_specs=pl.BlockSpec(memory_space=pltpu.VMEM),
            compiler_params=pltpu.CompilerParams(vmem_limit_bytes=4 * MIB),
            name="pair_rows",
        )(place, packed, ctx_permute(packed, dz=1))
    with jax.named_scope("rows_y"):
        block = jnp.concatenate([kv_rows[0].T, kv_tangent[0].T], axis=0)
        near_block, copies = lax.optimization_barrier((block, copies))
        rows = exchange(copies, "ctx", Y_GROUPS).reshape(row_count, packed_width)

    with jax.named_scope("keys_x"):
        far_block = ctx_permute(block, dx=2)
        near_blocks = [ctx_permute(near_block, dx=step) for step in (1, -1)]
        blocks = [block, near_blocks[0], far_block, near_blocks[1]]
    gains = (norm_gain[:, None], gain_tangent[:, None])
    keys = pl.pallas_call(
        keys_kernel,
        out_shape=jax.ShapeDtypeStruct((X, full_width, 2 * key_count), jnp.bfloat16),
        in_specs=in_vmem(2 + X),
        out_specs=pl.BlockSpec(memory_space=pltpu.VMEM),
        compiler_params=pltpu.CompilerParams(vmem_limit_bytes=8 * MIB),
        name="make_keys",
    )(*gains, *blocks)

    sums = pl.pallas_call(
        functools.partial(stats_kernel, slab),
        out_shape=jax.ShapeDtypeStruct((Y * ZH, SUMS, row_count // LANES, LANES), jnp.float32),
        in_specs=smem + in_vmem(2),
        out_specs=pl.BlockSpec(memory_space=pltpu.VMEM),
        compiler_params=pltpu.CompilerParams(vmem_limit_bytes=12 * MIB),
        cost_estimate=pl.CostEstimate(
            flops=flops, bytes_accessed=3 * MIB, transcendentals=X * key_count * row_count
        ),
        name="local_stats",
    )(place, keys, rows)
    with jax.named_scope("stats_yz"):
        sums = exchange(sums, "ctx", YZ_GROUPS)

    *shares, pair = pl.pallas_call(
        functools.partial(grads_kernel, slab),
        out_shape=[jax.ShapeDtypeStruct((full_width, key_count), jnp.float32)] * X
        + [jax.ShapeDtypeStruct((X * Y, SUBLANES, LANES), jnp.float32)],
        in_specs=smem + in_vmem(5 + X),
        out_specs=in_vmem(X + 1),
        compiler_params=pltpu.CompilerParams(vmem_limit_bytes=16 * MIB),
        cost_estimate=pl.CostEstimate(
            flops=2 * flops, bytes_accessed=6 * MIB, transcendentals=X * key_count * row_count
        ),
        name="gradients",
    )(place, sums, keys, rows, *gains, *blocks)

    with jax.named_scope("shares_x"):
        hv_rows = sum([ctx_permute(shares[step], dx=-step) for step in (2, 3, 1)], shares[0])
    with jax.named_scope("pair_plane"):
        pair = pl.pallas_call(
            add_kernel,
            out_shape=jax.ShapeDtypeStruct((Z * CORE, SUBLANES, LANES), jnp.float32),
            compiler_params=pltpu.CompilerParams(vmem_limit_bytes=2 * MIB),
            cost_estimate=pl.CostEstimate(
                flops=10**11, bytes_accessed=MIB // 4, transcendentals=0
            ),
            name="add_pair",
        )(exchange(pair, ("dp", "ctx"), PLANES))
    with jax.named_scope("pair_column"):
        pair = jnp.sum(exchange(pair, ("dp", "ctx"), COLUMNS), axis=0).reshape(2, latent_width)
    return (hv_rows.T[None], pair)


def solution(mesh):
    in_specs = (
        P("dp"),
        P("dp"),
        P("dp", None, "ctx", None),
        P("dp", None, "ctx", None),
        P("dp", "ctx", None),
        P("dp", "ctx", None),
        P(),
        P(),
    )
    out_specs = (P("dp", "ctx", None), P())
    return jax.shard_map(shards, mesh=mesh, in_specs=in_specs, out_specs=out_specs, check_vma=False)
```

```python
import functools

import jax
import jax.numpy as jnp
from jax import lax
from jax.experimental import pallas as pl
from jax.experimental.pallas import tpu as pltpu
from jax.sharding import PartitionSpec as P

score_scale = 192.0 ** (-0.5)
tiny_eps = 1e-06
masked_score = -1e30

X, Y, ZH = 4, 8, 2
ZL, CORE = 4, 2
CTX = X * Y * ZH
Z = ZH * ZL
LANES = 128
SUBLANES = 8
SUMS = 5
MIB = 2**20


def ctx_index(x, y, zh):
    return (x * Y + y) * ZH + zh


def device_index(x, y, z, core):
    return (z % ZL * CORE + core) * CTX + ctx_index(x, y, z // ZL)


Y_GROUPS = [[ctx_index(x, y, z) for y in range(Y)] for x in range(X) for z in range(ZH)]
YZ_GROUPS = [[ctx_index(x, y, z) for y in range(Y) for z in range(ZH)] for x in range(X)]
COLUMNS = [
    [device_index(x, y, z, core) for z in range(Z) for core in range(CORE)]
    for x in range(X)
    for y in range(Y)
]
PLANES = [
    [device_index(x, y, z, core) for x in range(X) for y in range(Y)]
    for z in range(Z)
    for core in range(CORE)
]


def ctx_permute(value, dx=0, dz=0):
    pairs = [
        (ctx_index(x, y, z), ctx_index((x + dx) % X, y, (z + dz) % ZH))
        for x in range(X)
        for y in range(Y)
        for z in range(ZH)
    ]
    return lax.ppermute(value, "ctx", pairs)


def exchange(copies, axis, groups=None):
    return lax.all_to_all(copies, axis, 0, 0, axis_index_groups=groups)


def dot(left, right):
    return jnp.dot(left, right, preferred_element_type=jnp.float32)


def pair_kernel(latent_width, place_ref, own_ref, other_ref, out_ref):
    z, live_count = place_ref[1], place_ref[3]
    shape = own_ref.shape
    row = lax.broadcasted_iota(jnp.int32, shape, 0)
    column = lax.broadcasted_iota(jnp.int32, shape, 1)
    kept = (row < live_count) | (column >= latent_width)
    for at, ref in ((z, own_ref), (1 - z, other_ref)):
        rows = jnp.where(kept, ref[...].astype(jnp.float32), 0.0).astype(ref.dtype)
        for copy in range(Y):
            out_ref[copy, at] = rows


def norm_side(block_ref, latent_width):
    full_width = block_ref.shape[0] // 2
    latent = block_ref[:latent_width, :].astype(jnp.float32)
    latent_dot = block_ref[full_width : full_width + latent_width, :].astype(jnp.float32)
    inv_rms = lax.rsqrt(jnp.mean(latent * latent, axis=0, keepdims=True) + tiny_eps)
    normed = latent * inv_rms
    inv_dot = -(inv_rms * inv_rms * inv_rms) * jnp.mean(latent * latent_dot, axis=0, keepdims=True)
    normed_dot = latent_dot * inv_rms + latent * inv_dot
    return (latent, latent_dot, inv_rms, inv_dot, normed, normed_dot)


def keys_kernel(gain_ref, gain_tangent_ref, *refs):
    *block_refs, keys_ref = refs
    latent_width, full_width = gain_ref.shape[0], keys_ref.shape[1]
    norm_gain, gain_tangent = gain_ref[...], gain_tangent_ref[...]
    for at, block_ref in enumerate(block_refs):
        normed, normed_dot = norm_side(block_ref, latent_width)[4:]
        count = block_ref.shape[1]
        keys_ref[at, :latent_width, :count] = (normed * norm_gain).astype(jnp.bfloat16)
        keys_ref[at, :latent_width, count:] = (
            gain_tangent * normed + norm_gain * normed_dot
        ).astype(jnp.bfloat16)
        keys_ref[at, latent_width:, :count] = block_ref[latent_width:full_width, :]
        keys_ref[at, latent_width:, count:] = block_ref[full_width + latent_width :, :]


def block_terms(behind, slab, place_ref, keys_ref, rows_ref):
    row_count, width = rows_ref.shape
    key_count = keys_ref.shape[2] // 2
    latent_width = width - keys_ref.shape[1]
    keys = keys_ref[behind]
    by_query = score_scale * dot(rows_ref[:, latent_width:], keys)
    by_cot = dot(rows_ref[:, :latent_width], keys[:latent_width])
    x = lax.rem(place_ref[0] + (X - behind), X)
    key_pos = (x * (Y * ZH) + place_ref[4]) * key_count
    key_pos += lax.broadcasted_iota(jnp.int32, (row_count, key_count), 1)
    slab_row = lax.broadcasted_iota(jnp.int32, (row_count, key_count), 0) % slab
    visible = key_pos <= place_ref[2] + slab_row
    return (
        by_query[:, :key_count],
        by_query[:, key_count:],
        by_cot[:, :key_count],
        by_cot[:, key_count:],
        visible,
    )


def as_rows(columns):
    shape = (columns[0].shape[0], LANES)
    lane = lax.broadcasted_iota(jnp.int32, shape, 1)
    filled = jnp.zeros(shape, jnp.float32)
    for at, column in enumerate(columns):
        filled = jnp.where(lane == at, column, filled)
    return filled.T[:SUBLANES]


def stats_kernel(slab, place_ref, keys_ref, rows_ref, out_ref):
    terms = [block_terms(behind, slab, place_ref, keys_ref, rows_ref) for behind in range(X)]
    maxima = [jnp.where(visible, scores, masked_score) for scores, _, _, _, visible in terms]
    maxima = jnp.max(functools.reduce(jnp.maximum, maxima), axis=1, keepdims=True)
    sums = [0.0] * 4
    for scores, score_dot, value_grad, value_dot, visible in terms:
        weights = jnp.where(visible, jnp.exp(scores - maxima), 0.0)
        sums[0] += weights
        sums[1] += weights * score_dot
        sums[2] += weights * value_grad
        sums[3] += weights * (score_dot * value_grad + value_dot)
    sums = as_rows([maxima] + [jnp.sum(each, axis=1, keepdims=True) for each in sums])
    for row in range(SUMS):
        values = sums[row : row + 1]
        values = jnp.concatenate([values[:, :LANES], values[:, LANES:]], axis=0)
        for copy in range(out_ref.shape[0]):
            out_ref[copy, row] = values


def merged_means(parts_ref):
    count = parts_ref.shape[0]
    maxima = functools.reduce(jnp.maximum, [parts_ref[at, 0] for at in range(count)])
    scales = [jnp.exp(parts_ref[at, 0] - maxima) for at in range(count)]
    sums = [
        sum(scales[at] * parts_ref[at, row] for at in range(count)) for row in range(1, SUMS)
    ]
    inv_totals = 1.0 / sums[0]
    shift_mean = sums[1] * inv_totals
    grad_mean = sums[2] * inv_totals
    grad_mean_dot = (sums[3] - shift_mean * sums[2]) * inv_totals
    rows = [
        jnp.concatenate([values[0:1], values[1:2]], axis=1)
        for values in (maxima, inv_totals, shift_mean, grad_mean, grad_mean_dot)
    ]
    rows.append(jnp.zeros((LANES - SUMS, 2 * LANES), jnp.float32))
    columns = jnp.concatenate(rows, axis=0).T
    return [columns[:, at : at + 1] for at in range(SUMS)]


def grads_kernel(slab, place_ref, parts_ref, keys_ref, rows_ref, *refs):
    gain_ref, gain_tangent_ref, block_refs = refs[0], refs[1], refs[2 : 2 + X]
    *share_refs, pair_ref, shares_ref, sems = refs[2 + X :]
    latent_width = gain_ref.shape[0]
    norm_gain, gain_tangent = gain_ref[...], gain_tangent_ref[...]
    turned_cot = rows_ref[:, :latent_width].T
    turned_query = rows_ref[:, latent_width:].T
    maxima, inv_totals, shift_mean, grad_mean, grad_mean_dot = merged_means(parts_ref)
    gain_grad = gain_grad_dot = 0.0
    writes = []
    for behind in (2, 3, 1, 0):
        scores, score_dot, value_grad, value_dot, visible = block_terms(
            behind, slab, place_ref, keys_ref, rows_ref
        )
        attention = jnp.where(visible, jnp.exp(scores - maxima), 0.0) * inv_totals
        attention_dot = attention * (score_dot - shift_mean)
        centred = value_grad - grad_mean
        score_grad = attention * centred
        score_grad_dot = attention_dot * centred + attention * (value_dot - grad_mean_dot)
        right = jnp.concatenate([score_grad, score_grad_dot], axis=1).astype(jnp.bfloat16)
        by_query = score_scale * dot(turned_query, right)
        right = jnp.concatenate([attention, attention_dot], axis=1).astype(jnp.bfloat16)
        by_cot = dot(turned_cot, right)

        key_count = scores.shape[1]
        latent_grad = by_query[:latent_width, :key_count] + by_cot[:, :key_count]
        latent_grad_dot = by_query[:latent_width, key_count:] + by_cot[:, key_count:]
        latent, latent_dot, inv_rms, inv_dot, normed, normed_dot = norm_side(
            block_refs[behind], latent_width
        )
        gain_grad += latent_grad * normed
        gain_grad_dot += latent_grad_dot * normed + latent_grad * normed_dot
        normed_grad = latent_grad * norm_gain
        normed_grad_dot = latent_grad_dot * norm_gain + latent_grad * gain_tangent
        inner_grad = jnp.mean(normed_grad * latent, axis=0, keepdims=True)
        inner_grad_dot = jnp.mean(
            normed_grad_dot * latent + normed_grad * latent_dot, axis=0, keepdims=True
        )
        rms_cubed = inv_rms * inv_rms * inv_rms
        rms_cubed_dot = 3.0 * inv_rms * inv_rms * inv_dot
        shares_ref[behind, :latent_width, :] = (
            inv_dot * normed_grad
            + inv_rms * normed_grad_dot
            - (rms_cubed_dot * inner_grad + rms_cubed * inner_grad_dot) * latent
            - (rms_cubed * inner_grad) * latent_dot
        )
        shares_ref[behind, latent_width:, :] = by_query[latent_width:, key_count:]
        write = pltpu.make_async_copy(shares_ref.at[behind], share_refs[behind], sems.at[behind])
        write.start()
        writes.append(write)
    pair = as_rows([jnp.sum(each, axis=1, keepdims=True) for each in (gain_grad, gain_grad_dot)])
    pair = jnp.concatenate(
        [
            pair[row : row + 1, at : at + LANES]
            for row in range(2)
            for at in range(0, latent_width, LANES)
        ],
        axis=0,
    )
    for copy in range(pair_ref.shape[0]):
        pair_ref[copy] = pair
    for write in writes:
        write.wait()


def add_kernel(parts_ref, out_ref):
    total = jnp.sum(parts_ref[...], axis=0)
    for copy in range(out_ref.shape[0]):
        out_ref[copy] = total


def in_vmem(count):
    return [pl.BlockSpec(memory_space=pltpu.VMEM)] * count


def shards(offsets, lengths, queries, cotangent, kv_rows, kv_tangent, norm_gain, gain_tangent):
    latent_width = norm_gain.shape[0]
    slab, full_width = queries.shape[1], queries.shape[3]
    key_count = kv_rows.shape[1]
    packed_width = latent_width + full_width
    row_count = Y * ZH * slab
    smem = [pl.BlockSpec(memory_space=pltpu.SMEM)]
    flops = 4 * X * key_count * row_count * packed_width
    ctx_at = lax.axis_index("ctx").astype(jnp.int32)
    place = jnp.stack(
        [
            ctx_at // (Y * ZH),
            ctx_at % ZH,
            offsets[0],
            lengths[0] - offsets[0],
            ctx_at % (Y * ZH),
        ]
    )

    packed = jnp.concatenate(
        [cotangent.reshape(slab, latent_width), queries.reshape(slab, full_width)], axis=1
    )
    with jax.named_scope("rows_z"):
        copies = pl.pallas_call(
            functools.partial(pair_kernel, latent_width),
            out_shape=jax.ShapeDtypeStruct((Y, ZH, slab, packed_width), packed.dtype),
            in_specs=smem + in_vmem(2),
            out_specs=pl.BlockSpec(memory_space=pltpu.VMEM),
            compiler_params=pltpu.CompilerParams(vmem_limit_bytes=4 * MIB),
            name="pair_rows",
        )(place, packed, ctx_permute(packed, dz=1))
    with jax.named_scope("rows_y"):
        block = jnp.concatenate([kv_rows[0].T, kv_tangent[0].T], axis=0)
        near_block, copies = lax.optimization_barrier((block, copies))
        rows = exchange(copies, "ctx", Y_GROUPS).reshape(row_count, packed_width)

    with jax.named_scope("keys_x"):
        far_block = ctx_permute(block, dx=2)
        near_blocks = [ctx_permute(near_block, dx=step) for step in (1, -1)]
        blocks = [block, near_blocks[0], far_block, near_blocks[1]]
    gains = (norm_gain[:, None], gain_tangent[:, None])
    keys = pl.pallas_call(
        keys_kernel,
        out_shape=jax.ShapeDtypeStruct((X, full_width, 2 * key_count), jnp.bfloat16),
        in_specs=in_vmem(2 + X),
        out_specs=pl.BlockSpec(memory_space=pltpu.VMEM),
        compiler_params=pltpu.CompilerParams(vmem_limit_bytes=8 * MIB),
        name="make_keys",
    )(*gains, *blocks)

    sums = pl.pallas_call(
        functools.partial(stats_kernel, slab),
        out_shape=jax.ShapeDtypeStruct((Y * ZH, SUMS, row_count // LANES, LANES), jnp.float32),
        in_specs=smem + in_vmem(2),
        out_specs=pl.BlockSpec(memory_space=pltpu.VMEM),
        compiler_params=pltpu.CompilerParams(vmem_limit_bytes=12 * MIB),
        cost_estimate=pl.CostEstimate(
            flops=flops, bytes_accessed=3 * MIB, transcendentals=X * key_count * row_count
        ),
        name="local_stats",
    )(place, keys, rows)
    with jax.named_scope("stats_yz"):
        sums = exchange(sums, "ctx", YZ_GROUPS)

    *shares, pair = pl.pallas_call(
        functools.partial(grads_kernel, slab),
        out_shape=[pltpu.HBM((full_width, key_count), jnp.float32)] * X
        + [jax.ShapeDtypeStruct((X * Y, SUBLANES, LANES), jnp.float32)],
        in_specs=smem + in_vmem(5 + X),
        out_specs=[pl.BlockSpec(memory_space=pltpu.HBM)] * X + in_vmem(1),
        scratch_shapes=[
            pltpu.VMEM((X, full_width, key_count), jnp.float32),
            pltpu.SemaphoreType.DMA((X,)),
        ],
        compiler_params=pltpu.CompilerParams(vmem_limit_bytes=16 * MIB),
        cost_estimate=pl.CostEstimate(
            flops=2 * flops, bytes_accessed=6 * MIB, transcendentals=X * key_count * row_count
        ),
        name="gradients",
    )(place, sums, keys, rows, *gains, *blocks)

    with jax.named_scope("shares_x"):
        hv_rows = sum([ctx_permute(shares[step], dx=-step) for step in (2, 3, 1)], shares[0])
    with jax.named_scope("pair_plane"):
        pair = pl.pallas_call(
            add_kernel,
            out_shape=jax.ShapeDtypeStruct((Z * CORE, SUBLANES, LANES), jnp.float32),
            compiler_params=pltpu.CompilerParams(vmem_limit_bytes=2 * MIB),
            cost_estimate=pl.CostEstimate(
                flops=10**11, bytes_accessed=MIB // 4, transcendentals=0
            ),
            name="add_pair",
        )(exchange(pair, ("dp", "ctx"), PLANES))
    with jax.named_scope("pair_column"):
        pair = jnp.sum(exchange(pair, ("dp", "ctx"), COLUMNS), axis=0).reshape(2, latent_width)
    return (hv_rows.T[None], pair)


def solution(mesh):
    in_specs = (
        P("dp"),
        P("dp"),
        P("dp", None, "ctx", None),
        P("dp", None, "ctx", None),
        P("dp", "ctx", None),
        P("dp", "ctx", None),
        P(),
        P(),
    )
    out_specs = (P("dp", "ctx", None), P())
    return jax.shard_map(shards, mesh=mesh, in_specs=in_specs, out_specs=out_specs, check_vma=False)
```

```python
import functools

import jax
import jax.numpy as jnp
from jax import lax
from jax.experimental import pallas as pl
from jax.experimental.pallas import tpu as pltpu
from jax.sharding import PartitionSpec as P

score_scale = 192.0 ** (-0.5)
tiny_eps = 1e-06
masked_score = -1e30

X, Y, ZH = 4, 8, 2
ZL, CORE = 4, 2
CTX = X * Y * ZH
Z = ZH * ZL
LANES = 128
SUBLANES = 8
SUMS = 5
MIB = 2**20


def ctx_index(x, y, zh):
    return (x * Y + y) * ZH + zh


def device_index(x, y, z, core):
    return (z % ZL * CORE + core) * CTX + ctx_index(x, y, z // ZL)


YZ_GROUPS = [[ctx_index(x, y, z) for y in range(Y) for z in range(ZH)] for x in range(X)]
COLUMNS = [
    [device_index(x, y, z, core) for z in range(Z) for core in range(CORE)]
    for x in range(X)
    for y in range(Y)
]
PLANES = [
    [device_index(x, y, z, core) for x in range(X) for y in range(Y)]
    for z in range(Z)
    for core in range(CORE)
]


def ctx_permute(value, dx):
    pairs = [
        (ctx_index(x, y, z), ctx_index((x + dx) % X, y, z))
        for x in range(X)
        for y in range(Y)
        for z in range(ZH)
    ]
    return lax.ppermute(value, "ctx", pairs)


def exchange(copies, axis, groups=None):
    return lax.all_to_all(copies, axis, 0, 0, axis_index_groups=groups)


def dot(left, right):
    return jnp.dot(left, right, preferred_element_type=jnp.float32)


def pack_kernel(place_ref, cot_ref, query_ref, out_ref):
    row = lax.broadcasted_iota(jnp.int32, cot_ref.shape, 0)
    cot = jnp.where(row < place_ref[2], cot_ref[...].astype(jnp.float32), 0.0)
    cot, query = cot.astype(cot_ref.dtype), query_ref[...]
    width = cot.shape[1]
    for copy in range(out_ref.shape[0]):
        out_ref[copy, :, :width] = cot
        out_ref[copy, :, width:] = query


def norm_side(block_ref, latent_width):
    full_width = block_ref.shape[0] // 2
    latent = block_ref[:latent_width, :].astype(jnp.float32)
    latent_dot = block_ref[full_width : full_width + latent_width, :].astype(jnp.float32)
    inv_rms = lax.rsqrt(jnp.mean(latent * latent, axis=0, keepdims=True) + tiny_eps)
    normed = latent * inv_rms
    inv_dot = -(inv_rms * inv_rms * inv_rms) * jnp.mean(latent * latent_dot, axis=0, keepdims=True)
    normed_dot = latent_dot * inv_rms + latent * inv_dot
    return (latent, latent_dot, inv_rms, inv_dot, normed, normed_dot)


def keys_kernel(gain_ref, gain_tangent_ref, *refs):
    *block_refs, keys_ref = refs
    latent_width, full_width = gain_ref.shape[0], keys_ref.shape[1]
    norm_gain, gain_tangent = gain_ref[...], gain_tangent_ref[...]
    for at, block_ref in enumerate(block_refs):
        normed, normed_dot = norm_side(block_ref, latent_width)[4:]
        count = block_ref.shape[1]
        keys_ref[at, :latent_width, :count] = (normed * norm_gain).astype(jnp.bfloat16)
        keys_ref[at, :latent_width, count:] = (
            gain_tangent * normed + norm_gain * normed_dot
        ).astype(jnp.bfloat16)
        keys_ref[at, latent_width:, :count] = block_ref[latent_width:full_width, :]
        keys_ref[at, latent_width:, count:] = block_ref[full_width + latent_width :, :]


def block_terms(behind, slab, place_ref, keys_ref, rows_ref):
    row_count, width = rows_ref.shape
    key_count = keys_ref.shape[2] // 2
    latent_width = width - keys_ref.shape[1]
    keys = keys_ref[behind]
    by_query = score_scale * dot(rows_ref[:, latent_width:], keys)
    by_cot = dot(rows_ref[:, :latent_width], keys[:latent_width])
    x = lax.rem(place_ref[0] + (X - behind), X)
    key_pos = (x * (Y * ZH) + place_ref[3]) * key_count
    key_pos += lax.broadcasted_iota(jnp.int32, (row_count, key_count), 1)
    slab_row = lax.broadcasted_iota(jnp.int32, (row_count, key_count), 0) % slab
    visible = key_pos <= place_ref[1] + slab_row
    return (
        by_query[:, :key_count],
        by_query[:, key_count:],
        by_cot[:, :key_count],
        by_cot[:, key_count:],
        visible,
    )


def as_rows(columns):
    shape = (columns[0].shape[0], LANES)
    lane = lax.broadcasted_iota(jnp.int32, shape, 1)
    filled = jnp.zeros(shape, jnp.float32)
    for at, column in enumerate(columns):
        filled = jnp.where(lane == at, column, filled)
    return filled.T[:SUBLANES]


def stats_kernel(slab, place_ref, keys_ref, rows_ref, out_ref):
    terms = [block_terms(behind, slab, place_ref, keys_ref, rows_ref) for behind in range(X)]
    maxima = [jnp.where(visible, scores, masked_score) for scores, _, _, _, visible in terms]
    maxima = jnp.max(functools.reduce(jnp.maximum, maxima), axis=1, keepdims=True)
    sums = [0.0] * 4
    for scores, score_dot, value_grad, value_dot, visible in terms:
        weights = jnp.where(visible, jnp.exp(scores - maxima), 0.0)
        sums[0] += weights
        sums[1] += weights * score_dot
        sums[2] += weights * value_grad
        sums[3] += weights * (score_dot * value_grad + value_dot)
    sums = as_rows([maxima] + [jnp.sum(each, axis=1, keepdims=True) for each in sums])
    for row in range(SUMS):
        values = sums[row : row + 1]
        values = jnp.concatenate([values[:, :LANES], values[:, LANES:]], axis=0)
        for copy in range(out_ref.shape[0]):
            out_ref[copy, row] = values


def merged_means(parts_ref):
    count = parts_ref.shape[0]
    maxima = functools.reduce(jnp.maximum, [parts_ref[at, 0] for at in range(count)])
    scales = [jnp.exp(parts_ref[at, 0] - maxima) for at in range(count)]
    sums = [
        sum(scales[at] * parts_ref[at, row] for at in range(count)) for row in range(1, SUMS)
    ]
    inv_totals = 1.0 / sums[0]
    shift_mean = sums[1] * inv_totals
    grad_mean = sums[2] * inv_totals
    grad_mean_dot = (sums[3] - shift_mean * sums[2]) * inv_totals
    rows = [
        jnp.concatenate([values[0:1], values[1:2]], axis=1)
        for values in (maxima, inv_totals, shift_mean, grad_mean, grad_mean_dot)
    ]
    rows.append(jnp.zeros((LANES - SUMS, 2 * LANES), jnp.float32))
    columns = jnp.concatenate(rows, axis=0).T
    return [columns[:, at : at + 1] for at in range(SUMS)]


def grads_kernel(slab, place_ref, parts_ref, keys_ref, rows_ref, *refs):
    gain_ref, gain_tangent_ref, block_refs = refs[0], refs[1], refs[2 : 2 + X]
    *share_refs, pair_ref, shares_ref, sems = refs[2 + X :]
    latent_width = gain_ref.shape[0]
    norm_gain, gain_tangent = gain_ref[...], gain_tangent_ref[...]
    turned_cot = rows_ref[:, :latent_width].T
    turned_query = rows_ref[:, latent_width:].T
    maxima, inv_totals, shift_mean, grad_mean, grad_mean_dot = merged_means(parts_ref)
    gain_grad = gain_grad_dot = 0.0
    writes = []
    for behind in (2, 3, 1, 0):
        scores, score_dot, value_grad, value_dot, visible = block_terms(
            behind, slab, place_ref, keys_ref, rows_ref
        )
        attention = jnp.where(visible, jnp.exp(scores - maxima), 0.0) * inv_totals
        attention_dot = attention * (score_dot - shift_mean)
        centred = value_grad - grad_mean
        score_grad = attention * centred
        score_grad_dot = attention_dot * centred + attention * (value_dot - grad_mean_dot)
        right = jnp.concatenate([score_grad, score_grad_dot], axis=1).astype(jnp.bfloat16)
        by_query = score_scale * dot(turned_query, right)
        right = jnp.concatenate([attention, attention_dot], axis=1).astype(jnp.bfloat16)
        by_cot = dot(turned_cot, right)

        key_count = scores.shape[1]
        latent_grad = by_query[:latent_width, :key_count] + by_cot[:, :key_count]
        latent_grad_dot = by_query[:latent_width, key_count:] + by_cot[:, key_count:]
        latent, latent_dot, inv_rms, inv_dot, normed, normed_dot = norm_side(
            block_refs[behind], latent_width
        )
        gain_grad += latent_grad * normed
        gain_grad_dot += latent_grad_dot * normed + latent_grad * normed_dot
        normed_grad = latent_grad * norm_gain
        normed_grad_dot = latent_grad_dot * norm_gain + latent_grad * gain_tangent
        inner_grad = jnp.mean(normed_grad * latent, axis=0, keepdims=True)
        inner_grad_dot = jnp.mean(
            normed_grad_dot * latent + normed_grad * latent_dot, axis=0, keepdims=True
        )
        rms_cubed = inv_rms * inv_rms * inv_rms
        rms_cubed_dot = 3.0 * inv_rms * inv_rms * inv_dot
        shares_ref[behind, :latent_width, :] = (
            inv_dot * normed_grad
            + inv_rms * normed_grad_dot
            - (rms_cubed_dot * inner_grad + rms_cubed * inner_grad_dot) * latent
            - (rms_cubed * inner_grad) * latent_dot
        )
        shares_ref[behind, latent_width:, :] = by_query[latent_width:, key_count:]
        write = pltpu.make_async_copy(shares_ref.at[behind], share_refs[behind], sems.at[behind])
        write.start()
        writes.append(write)
    pair = as_rows([jnp.sum(each, axis=1, keepdims=True) for each in (gain_grad, gain_grad_dot)])
    pair = jnp.concatenate(
        [
            pair[row : row + 1, at : at + LANES]
            for row in range(2)
            for at in range(0, latent_width, LANES)
        ],
        axis=0,
    )
    for copy in range(pair_ref.shape[0]):
        pair_ref[copy] = pair
    for write in writes:
        write.wait()


def add_kernel(parts_ref, out_ref):
    total = jnp.sum(parts_ref[...], axis=0)
    for copy in range(out_ref.shape[0]):
        out_ref[copy] = total


def in_vmem(count):
    return [pl.BlockSpec(memory_space=pltpu.VMEM)] * count


def shards(offsets, lengths, queries, cotangent, kv_rows, kv_tangent, norm_gain, gain_tangent):
    latent_width = norm_gain.shape[0]
    slab, full_width = queries.shape[1], queries.shape[3]
    key_count = kv_rows.shape[1]
    packed_width = latent_width + full_width
    row_count = Y * ZH * slab
    smem = [pl.BlockSpec(memory_space=pltpu.SMEM)]
    flops = 4 * X * key_count * row_count * packed_width
    ctx_at = lax.axis_index("ctx").astype(jnp.int32)
    place = jnp.stack(
        [
            ctx_at // (Y * ZH),
            offsets[0],
            lengths[0] - offsets[0],
            ctx_at % (Y * ZH),
        ]
    )

    with jax.named_scope("rows_yz"):
        copies = pl.pallas_call(
            pack_kernel,
            out_shape=jax.ShapeDtypeStruct((Y * ZH, slab, packed_width), queries.dtype),
            in_specs=smem + in_vmem(2),
            out_specs=pl.BlockSpec(memory_space=pltpu.VMEM),
            compiler_params=pltpu.CompilerParams(vmem_limit_bytes=4 * MIB),
            name="pack_rows",
        )(place, cotangent.reshape(slab, latent_width), queries.reshape(slab, full_width))
        block = jnp.concatenate([kv_rows[0].T, kv_tangent[0].T], axis=0)
        near_block, copies = lax.optimization_barrier((block, copies))
        rows = exchange(copies, "ctx", YZ_GROUPS).reshape(row_count, packed_width)

    with jax.named_scope("keys_x"):
        far_block = ctx_permute(block, dx=2)
        near_blocks = [ctx_permute(near_block, dx=step) for step in (1, -1)]
        blocks = [block, near_blocks[0], far_block, near_blocks[1]]
    gains = (norm_gain[:, None], gain_tangent[:, None])
    keys = pl.pallas_call(
        keys_kernel,
        out_shape=jax.ShapeDtypeStruct((X, full_width, 2 * key_count), jnp.bfloat16),
        in_specs=in_vmem(2 + X),
        out_specs=pl.BlockSpec(memory_space=pltpu.VMEM),
        compiler_params=pltpu.CompilerParams(vmem_limit_bytes=8 * MIB),
        name="make_keys",
    )(*gains, *blocks)

    sums = pl.pallas_call(
        functools.partial(stats_kernel, slab),
        out_shape=jax.ShapeDtypeStruct((Y * ZH, SUMS, row_count // LANES, LANES), jnp.float32),
        in_specs=smem + in_vmem(2),
        out_specs=pl.BlockSpec(memory_space=pltpu.VMEM),
        compiler_params=pltpu.CompilerParams(vmem_limit_bytes=12 * MIB),
        cost_estimate=pl.CostEstimate(
            flops=flops, bytes_accessed=3 * MIB, transcendentals=X * key_count * row_count
        ),
        name="local_stats",
    )(place, keys, rows)
    with jax.named_scope("stats_yz"):
        sums = exchange(sums, "ctx", YZ_GROUPS)

    *shares, pair = pl.pallas_call(
        functools.partial(grads_kernel, slab),
        out_shape=[pltpu.HBM((full_width, key_count), jnp.float32)] * X
        + [jax.ShapeDtypeStruct((X * Y, SUBLANES, LANES), jnp.float32)],
        in_specs=smem + in_vmem(5 + X),
        out_specs=[pl.BlockSpec(memory_space=pltpu.HBM)] * X + in_vmem(1),
        scratch_shapes=[
            pltpu.VMEM((X, full_width, key_count), jnp.float32),
            pltpu.SemaphoreType.DMA((X,)),
        ],
        compiler_params=pltpu.CompilerParams(vmem_limit_bytes=16 * MIB),
        cost_estimate=pl.CostEstimate(
            flops=2 * flops, bytes_accessed=6 * MIB, transcendentals=X * key_count * row_count
        ),
        name="gradients",
    )(place, sums, keys, rows, *gains, *blocks)

    with jax.named_scope("shares_x"):
        hv_rows = sum([ctx_permute(shares[step], dx=-step) for step in (2, 3, 1)], shares[0])
    with jax.named_scope("pair_plane"):
        pair = pl.pallas_call(
            add_kernel,
            out_shape=jax.ShapeDtypeStruct((Z * CORE, SUBLANES, LANES), jnp.float32),
            compiler_params=pltpu.CompilerParams(vmem_limit_bytes=2 * MIB),
            cost_estimate=pl.CostEstimate(
                flops=10**11, bytes_accessed=MIB // 4, transcendentals=0
            ),
            name="add_pair",
        )(exchange(pair, ("dp", "ctx"), PLANES))
    with jax.named_scope("pair_column"):
        pair = jnp.sum(exchange(pair, ("dp", "ctx"), COLUMNS), axis=0).reshape(2, latent_width)
    return (hv_rows.T[None], pair)


def solution(mesh):
    in_specs = (
        P("dp"),
        P("dp"),
        P("dp", None, "ctx", None),
        P("dp", None, "ctx", None),
        P("dp", "ctx", None),
        P("dp", "ctx", None),
        P(),
        P(),
    )
    out_specs = (P("dp", "ctx", None), P())
    return jax.shard_map(shards, mesh=mesh, in_specs=in_specs, out_specs=out_specs, check_vma=False)
```

```python
import functools

import jax
import jax.numpy as jnp
from jax import lax
from jax.experimental import pallas as pl
from jax.experimental.pallas import tpu as pltpu
from jax.sharding import PartitionSpec as P

score_scale = 192.0 ** (-0.5)
tiny_eps = 1e-06
masked_score = -1e30

X, Y, ZH = 4, 8, 2
ZL, CORE = 4, 2
CTX = X * Y * ZH
Z = ZH * ZL
LANES = 128
SUBLANES = 8
SUMS = 5
MIB = 2**20


def ctx_index(x, y, zh):
    return (x * Y + y) * ZH + zh


def device_index(x, y, z, core):
    return (z % ZL * CORE + core) * CTX + ctx_index(x, y, z // ZL)


YZ_GROUPS = [[ctx_index(x, y, z) for y in range(Y) for z in range(ZH)] for x in range(X)]
COLUMNS = [
    [device_index(x, y, z, core) for z in range(Z) for core in range(CORE)]
    for x in range(X)
    for y in range(Y)
]
PLANES = [
    [device_index(x, y, z, core) for x in range(X) for y in range(Y)]
    for z in range(Z)
    for core in range(CORE)
]


def ctx_permute(value, dx):
    pairs = [
        (ctx_index(x, y, z), ctx_index((x + dx) % X, y, z))
        for x in range(X)
        for y in range(Y)
        for z in range(ZH)
    ]
    return lax.ppermute(value, "ctx", pairs)


def exchange(copies, axis, groups=None):
    return lax.all_to_all(copies, axis, 0, 0, axis_index_groups=groups)


def dot(left, right):
    return jnp.dot(left, right, preferred_element_type=jnp.float32)


def pack_kernel(place_ref, cot_ref, query_ref, out_ref):
    row = lax.broadcasted_iota(jnp.int32, cot_ref.shape, 0)
    cot = jnp.where(row < place_ref[2], cot_ref[...].astype(jnp.float32), 0.0)
    cot, query = cot.astype(cot_ref.dtype), query_ref[...]
    width = cot.shape[1]
    for copy in range(out_ref.shape[0]):
        out_ref[copy, :, :width] = cot
        out_ref[copy, :, width:] = query


def norm_side(block_ref, latent_width):
    full_width = block_ref.shape[0] // 2
    latent = block_ref[:latent_width, :].astype(jnp.float32)
    latent_dot = block_ref[full_width : full_width + latent_width, :].astype(jnp.float32)
    inv_rms = lax.rsqrt(jnp.mean(latent * latent, axis=0, keepdims=True) + tiny_eps)
    normed = latent * inv_rms
    inv_dot = -(inv_rms * inv_rms * inv_rms) * jnp.mean(latent * latent_dot, axis=0, keepdims=True)
    normed_dot = latent_dot * inv_rms + latent * inv_dot
    return (latent, latent_dot, inv_rms, inv_dot, normed, normed_dot)


def keys_kernel(gain_ref, gain_tangent_ref, *refs):
    *block_refs, keys_ref = refs
    latent_width, full_width = gain_ref.shape[0], keys_ref.shape[1]
    norm_gain, gain_tangent = gain_ref[...], gain_tangent_ref[...]
    for at, block_ref in enumerate(block_refs):
        normed, normed_dot = norm_side(block_ref, latent_width)[4:]
        count = block_ref.shape[1]
        keys_ref[at, :latent_width, :count] = (normed * norm_gain).astype(jnp.bfloat16)
        keys_ref[at, :latent_width, count:] = (
            gain_tangent * normed + norm_gain * normed_dot
        ).astype(jnp.bfloat16)
        keys_ref[at, latent_width:, :count] = block_ref[latent_width:full_width, :]
        keys_ref[at, latent_width:, count:] = block_ref[full_width + latent_width :, :]


def block_terms(behind, slab, place_ref, keys_ref, rows_ref):
    row_count, width = rows_ref.shape
    key_count = keys_ref.shape[2] // 2
    latent_width = width - keys_ref.shape[1]
    keys = keys_ref[behind]
    by_query = score_scale * dot(rows_ref[:, latent_width:], keys)
    by_cot = dot(rows_ref[:, :latent_width], keys[:latent_width])
    x = lax.rem(place_ref[0] + (X - behind), X)
    key_pos = (x * (Y * ZH) + place_ref[3]) * key_count
    key_pos += lax.broadcasted_iota(jnp.int32, (row_count, key_count), 1)
    slab_row = lax.broadcasted_iota(jnp.int32, (row_count, key_count), 0) % slab
    visible = key_pos <= place_ref[1] + slab_row
    return (
        by_query[:, :key_count],
        by_query[:, key_count:],
        by_cot[:, :key_count],
        by_cot[:, key_count:],
        visible,
    )


def as_rows(columns):
    shape = (columns[0].shape[0], LANES)
    lane = lax.broadcasted_iota(jnp.int32, shape, 1)
    filled = jnp.zeros(shape, jnp.float32)
    for at, column in enumerate(columns):
        filled = jnp.where(lane == at, column, filled)
    return filled.T[:SUBLANES]


def stats_kernel(slab, place_ref, keys_ref, rows_ref, out_ref):
    terms = [block_terms(behind, slab, place_ref, keys_ref, rows_ref) for behind in range(X)]
    maxima = [jnp.where(visible, scores, masked_score) for scores, _, _, _, visible in terms]
    maxima = jnp.max(functools.reduce(jnp.maximum, maxima), axis=1, keepdims=True)
    sums = [0.0] * 4
    for scores, score_dot, value_grad, value_dot, visible in terms:
        weights = jnp.where(visible, jnp.exp(scores - maxima), 0.0)
        sums[0] += weights
        sums[1] += weights * score_dot
        sums[2] += weights * value_grad
        sums[3] += weights * (score_dot * value_grad + value_dot)
    sums = as_rows([maxima] + [jnp.sum(each, axis=1, keepdims=True) for each in sums])
    for row in range(SUMS):
        values = sums[row : row + 1]
        values = jnp.concatenate([values[:, :LANES], values[:, LANES:]], axis=0)
        for copy in range(out_ref.shape[0]):
            out_ref[copy, row] = values


def merged_means(parts_ref):
    count = parts_ref.shape[0]
    maxima = functools.reduce(jnp.maximum, [parts_ref[at, 0] for at in range(count)])
    scales = [jnp.exp(parts_ref[at, 0] - maxima) for at in range(count)]
    sums = [
        sum(scales[at] * parts_ref[at, row] for at in range(count)) for row in range(1, SUMS)
    ]
    inv_totals = 1.0 / sums[0]
    shift_mean = sums[1] * inv_totals
    grad_mean = sums[2] * inv_totals
    grad_mean_dot = (sums[3] - shift_mean * sums[2]) * inv_totals
    rows = [
        jnp.concatenate([values[0:1], values[1:2]], axis=1)
        for values in (maxima, inv_totals, shift_mean, grad_mean, grad_mean_dot)
    ]
    rows.append(jnp.zeros((LANES - SUMS, 2 * LANES), jnp.float32))
    columns = jnp.concatenate(rows, axis=0).T
    return [columns[:, at : at + 1] for at in range(SUMS)]


def grads_kernel(slab, place_ref, parts_ref, keys_ref, rows_ref, *refs):
    gain_ref, gain_tangent_ref, block_refs = refs[0], refs[1], refs[2 : 2 + X]
    *share_refs, pair_ref, shares_ref, sems = refs[2 + X :]
    latent_width = gain_ref.shape[0]
    norm_gain, gain_tangent = gain_ref[...], gain_tangent_ref[...]
    turned_cot = rows_ref[:, :latent_width].T
    turned_query = rows_ref[:, latent_width:].T
    maxima, inv_totals, shift_mean, grad_mean, grad_mean_dot = merged_means(parts_ref)
    gain_grad = gain_grad_dot = 0.0
    writes = []
    for behind in (2, 3, 1, 0):
        scores, score_dot, value_grad, value_dot, visible = block_terms(
            behind, slab, place_ref, keys_ref, rows_ref
        )
        attention = jnp.where(visible, jnp.exp(scores - maxima), 0.0) * inv_totals
        attention_dot = attention * (score_dot - shift_mean)
        centred = value_grad - grad_mean
        score_grad = attention * centred
        score_grad_dot = attention_dot * centred + attention * (value_dot - grad_mean_dot)
        right = jnp.concatenate([score_grad, score_grad_dot], axis=1).astype(jnp.bfloat16)
        by_query = score_scale * dot(turned_query, right)
        right = jnp.concatenate([attention, attention_dot], axis=1).astype(jnp.bfloat16)
        by_cot = dot(turned_cot, right)

        key_count = scores.shape[1]
        latent_grad = by_query[:latent_width, :key_count] + by_cot[:, :key_count]
        latent_grad_dot = by_query[:latent_width, key_count:] + by_cot[:, key_count:]
        latent, latent_dot, inv_rms, inv_dot, normed, normed_dot = norm_side(
            block_refs[behind], latent_width
        )
        gain_grad += latent_grad * normed
        gain_grad_dot += latent_grad_dot * normed + latent_grad * normed_dot
        normed_grad = latent_grad * norm_gain
        normed_grad_dot = latent_grad_dot * norm_gain + latent_grad * gain_tangent
        inner_grad = jnp.mean(normed_grad * latent, axis=0, keepdims=True)
        inner_grad_dot = jnp.mean(
            normed_grad_dot * latent + normed_grad * latent_dot, axis=0, keepdims=True
        )
        rms_cubed = inv_rms * inv_rms * inv_rms
        rms_cubed_dot = 3.0 * inv_rms * inv_rms * inv_dot
        shares_ref[behind, :latent_width, :] = (
            inv_dot * normed_grad
            + inv_rms * normed_grad_dot
            - (rms_cubed_dot * inner_grad + rms_cubed * inner_grad_dot) * latent
            - (rms_cubed * inner_grad) * latent_dot
        )
        shares_ref[behind, latent_width:, :] = by_query[latent_width:, key_count:]
        write = pltpu.make_async_copy(shares_ref.at[behind], share_refs[behind], sems.at[behind])
        write.start()
        writes.append(write)
    pair = as_rows([jnp.sum(each, axis=1, keepdims=True) for each in (gain_grad, gain_grad_dot)])
    pair = jnp.concatenate(
        [
            pair[row : row + 1, at : at + LANES]
            for row in range(2)
            for at in range(0, latent_width, LANES)
        ],
        axis=0,
    )
    for copy in range(pair_ref.shape[0]):
        pair_ref[copy] = pair
    for write in writes:
        write.wait()


def add_kernel(parts_ref, out_ref):
    total = jnp.sum(parts_ref[...], axis=0)
    for copy in range(out_ref.shape[0]):
        out_ref[copy] = total


def in_vmem(count):
    return [pl.BlockSpec(memory_space=pltpu.VMEM)] * count


def shards(offsets, lengths, queries, cotangent, kv_rows, kv_tangent, norm_gain, gain_tangent):
    latent_width = norm_gain.shape[0]
    slab, full_width = queries.shape[1], queries.shape[3]
    key_count = kv_rows.shape[1]
    packed_width = latent_width + full_width
    row_count = Y * ZH * slab
    smem = [pl.BlockSpec(memory_space=pltpu.SMEM)]
    flops = 4 * X * key_count * row_count * packed_width
    ctx_at = lax.axis_index("ctx").astype(jnp.int32)
    place = jnp.stack(
        [
            ctx_at // (Y * ZH),
            offsets[0],
            lengths[0] - offsets[0],
            ctx_at % (Y * ZH),
        ]
    )

    with jax.named_scope("rows_yz"):
        copies = pl.pallas_call(
            pack_kernel,
            out_shape=jax.ShapeDtypeStruct((Y * ZH, slab, packed_width), queries.dtype),
            in_specs=smem + in_vmem(2),
            out_specs=pl.BlockSpec(memory_space=pltpu.VMEM),
            name="pack_rows",
        )(place, cotangent.reshape(slab, latent_width), queries.reshape(slab, full_width))
        kv_rows, kv_tangent, copies = lax.optimization_barrier((kv_rows, kv_tangent, copies))
        block = jnp.concatenate([kv_rows[0].T, kv_tangent[0].T], axis=0)
        rows = exchange(copies, "ctx", YZ_GROUPS).reshape(row_count, packed_width)

    with jax.named_scope("keys_x"):
        far_block = ctx_permute(block, dx=2)
        near_blocks = [ctx_permute(block, dx=step) for step in (1, -1)]
        blocks = [block, near_blocks[0], far_block, near_blocks[1]]
    gains = (norm_gain[:, None], gain_tangent[:, None])
    keys = pl.pallas_call(
        keys_kernel,
        out_shape=jax.ShapeDtypeStruct((X, full_width, 2 * key_count), jnp.bfloat16),
        in_specs=in_vmem(2 + X),
        out_specs=pl.BlockSpec(memory_space=pltpu.VMEM),
        compiler_params=pltpu.CompilerParams(vmem_limit_bytes=8 * MIB),
        name="make_keys",
    )(*gains, *blocks)

    sums = pl.pallas_call(
        functools.partial(stats_kernel, slab),
        out_shape=jax.ShapeDtypeStruct((Y * ZH, SUMS, row_count // LANES, LANES), jnp.float32),
        in_specs=smem + in_vmem(2),
        out_specs=pl.BlockSpec(memory_space=pltpu.VMEM),
        compiler_params=pltpu.CompilerParams(vmem_limit_bytes=12 * MIB),
        cost_estimate=pl.CostEstimate(
            flops=flops, bytes_accessed=3 * MIB, transcendentals=X * key_count * row_count
        ),
        name="local_stats",
    )(place, keys, rows)
    with jax.named_scope("stats_yz"):
        sums = exchange(sums, "ctx", YZ_GROUPS)

    *shares, pair = pl.pallas_call(
        functools.partial(grads_kernel, slab),
        out_shape=[pltpu.HBM((full_width, key_count), jnp.float32)] * X
        + [jax.ShapeDtypeStruct((X * Y, SUBLANES, LANES), jnp.float32)],
        in_specs=smem + in_vmem(5 + X),
        out_specs=[pl.BlockSpec(memory_space=pltpu.HBM)] * X + in_vmem(1),
        scratch_shapes=[
            pltpu.VMEM((X, full_width, key_count), jnp.float32),
            pltpu.SemaphoreType.DMA((X,)),
        ],
        compiler_params=pltpu.CompilerParams(vmem_limit_bytes=16 * MIB),
        cost_estimate=pl.CostEstimate(
            flops=2 * flops, bytes_accessed=6 * MIB, transcendentals=X * key_count * row_count
        ),
        name="gradients",
    )(place, sums, keys, rows, *gains, *blocks)

    with jax.named_scope("shares_x"):
        hv_rows = sum([ctx_permute(shares[step], dx=-step) for step in (2, 3, 1)], shares[0])
    with jax.named_scope("pair_plane"):
        pair = pl.pallas_call(
            add_kernel,
            out_shape=jax.ShapeDtypeStruct((Z * CORE, SUBLANES, LANES), jnp.float32),
            compiler_params=pltpu.CompilerParams(vmem_limit_bytes=2 * MIB),
            cost_estimate=pl.CostEstimate(
                flops=10**11, bytes_accessed=MIB // 4, transcendentals=0
            ),
            name="add_pair",
        )(exchange(pair, ("dp", "ctx"), PLANES))
    with jax.named_scope("pair_column"):
        pair = jnp.sum(exchange(pair, ("dp", "ctx"), COLUMNS), axis=0).reshape(2, latent_width)
    return (hv_rows.T[None], pair)


def solution(mesh):
    in_specs = (
        P("dp"),
        P("dp"),
        P("dp", None, "ctx", None),
        P("dp", None, "ctx", None),
        P("dp", "ctx", None),
        P("dp", "ctx", None),
        P(),
        P(),
    )
    out_specs = (P("dp", "ctx", None), P())
    return jax.shard_map(shards, mesh=mesh, in_specs=in_specs, out_specs=out_specs, check_vma=False)
```
